128 devices in a mesh: row: 16 (over y_hi, x, core), col: 8 (over y_lo, z).
Axes of the slice: x: 4, y: 4 (y_hi: 2, y_lo: 2; y = y_hi * 2 + y_lo), z: 4, core: 2. Of those that a mesh axis runs over, the one named last changes fastest.
Arguments:
- genotypes: int32 [32768, 512], P(('row', 'col')), may hold values from 0 to 2, as said below
- pairs: int32 [128, 2, 2], replicated, may hold values from -1 to 15, as said below
Outputs:
- relation: bfloat16 [128, 2, 2048, 2048], P(('row', 'col'))
The draws below stay inside these ranges and needn't reach their ends.
Inputs may be any that keep to these rules, and one draw needn't show every extreme that they name: `genotypes`: allele counts of one individual at one variant. `pairs`: each pair (r, j) of blocks with 0 <= j <= r < 16 stands in exactly one slot, as (r, j); every other slot holds (-1, -1).
All inputs are finite; a program needn't handle non-finite values.
Results may differ from the reference program's by a relative error of at most 0.0051.
Values may be sent and summed in bfloat16 or wider, within the bound.
A program may use at most 192 MiB of HBM per device.

```python
import jax
import jax.numpy as jnp
from jax import lax

SNPS = 512
BLOCK = 2048
SAMPLES = 32768
N_ROW = 16


def draw_genotypes(key, part):
    key = jax.random.fold_in(key, 7)
    key_base, key_first, key_second = jax.random.split(key, 3)
    base_rate = jax.random.randint(key_base, (SNPS,), 20, 200)
    nblocks = SAMPLES // BLOCK
    block_of = jnp.arange(SAMPLES, dtype=jnp.int32) // BLOCK
    level_rate = base_rate[None, :] * (nblocks - 1 + 2 * block_of[:, None]) // (nblocks - 1)
    first = jax.random.randint(key_first, (SAMPLES, SNPS), 0, 1000) < level_rate
    second = jax.random.randint(key_second, (SAMPLES, SNPS), 0, 1000) < level_rate
    return first.astype(jnp.int32) + second.astype(jnp.int32)


def draw_pairs(key, part):
    key = jax.random.fold_in(key, 11)
    nblocks = SAMPLES // BLOCK
    slot_index = jnp.arange(nblocks * nblocks, dtype=jnp.int32)
    row_block = slot_index // nblocks
    col_block = slot_index % nblocks
    is_lower = col_block <= row_block
    row_block = jnp.where(is_lower, row_block, -1)
    col_block = jnp.where(is_lower, col_block, -1)
    order = jax.random.permutation(key, nblocks * nblocks)
    stacked = jnp.stack([row_block[order], col_block[order]], axis=-1)
    return stacked.reshape(nblocks * nblocks // 2, 2, 2).astype(jnp.int32)


def setup_inputs(seed: int = 0) -> dict:
    key_of = jax.random.split(jax.random.key(seed), 3)
    genotypes = draw_genotypes(jax.random.fold_in(key_of[2], 71), 0)
    pairs = draw_pairs(jax.random.fold_in(key_of[2], 71), 0)
    return dict(genotypes=genotypes, pairs=pairs)


def reference(genotypes, pairs):
    counts = genotypes.astype(jnp.float32)
    mean_value = lax.optimization_barrier(jnp.sum(counts, axis=0)) / SAMPLES
    centered = counts - mean_value
    variance = lax.optimization_barrier(jnp.sum(centered * centered, axis=0)) / SAMPLES + 1e-05
    standard = (centered * lax.rsqrt(variance)).astype(jnp.bfloat16)
    blocks = standard.reshape(N_ROW, BLOCK, SNPS)

    def filled(slot_pair):
        left_panel = lax.dynamic_index_in_dim(blocks, slot_pair[0], 0, keepdims=False)
        right_panel = lax.dynamic_index_in_dim(blocks, slot_pair[1], 0, keepdims=False)
        product = jnp.dot(left_panel, right_panel.T, preferred_element_type=jnp.float32) / SNPS
        return product.astype(jnp.bfloat16)

    def vacant(slot_pair):
        return jnp.zeros((BLOCK, BLOCK), jnp.bfloat16)

    def one_slot(slot_pair):
        return lax.cond(slot_pair[0] >= 0, filled, vacant, slot_pair)
    slot_tiles = lax.map(one_slot, pairs.reshape(-1, 2))
    return slot_tiles.reshape(pairs.shape[0], 2, BLOCK, BLOCK)
```

```python
import functools
import itertools
import random

import jax
import jax.numpy as jnp
from jax import lax
from jax.experimental import pallas as pl
from jax.experimental.pallas import tpu as pltpu
from jax.sharding import PartitionSpec as P

MESH = pl.DeviceIdType.MESH
SNPS = 512
RING = 4
ROW_COUNT = 16
COL_COUNT = 8
SHARD = 256
SAMPLES = SHARD * ROW_COUNT * COL_COUNT
BLOCK = SHARD * COL_COUNT
PARTS = 2
PIECE = SHARD // PARTS
LINKS = ((1, 0, 0), (3, 0, 0), (0, 1, 0), (0, 3, 0), (0, 0, 1), (0, 0, 3))
OFFSETS = tuple(itertools.product(range(RING), repeat=3))
STAT_HOPS = {0: ("core",), 1: (1, 0, 0), 2: (0, 1, 0), 3: (0, 0, 1)}
CHUNK = 256


def plus(a, b):
    return tuple((i + j) % RING for i, j in zip(a, b))


def minus(a, b):
    return tuple((i - j) % RING for i, j in zip(a, b))


def number(offset):
    return (offset[0] * RING + offset[1]) * RING + offset[2]


def hops(offset):
    return sum(min(i, RING - i) for i in offset)


def attempt(seed, lag):
    rnd = random.Random(seed)
    have = {(p, (0, 0, 0)): -lag for p in range(PARTS)}
    steps = []
    for t in range((len(OFFSETS) - 1) * PARTS // len(LINKS)):
        choices = []
        for link in LINKS:
            ready = [
                (p, d)
                for p in range(PARTS)
                for d in OFFSETS
                if (p, d) not in have and have.get((p, minus(d, link)), t) <= t - lag
            ]
            rnd.shuffle(ready)
            ready.sort(key=lambda job: hops(job[1]))
            choices.append(ready)
        taken = {}

        def place(link, seen):
            for job in choices[link]:
                if job not in seen:
                    seen.add(job)
                    if job not in taken or place(taken[job], seen):
                        taken[job] = link
                        return True
            return False

        for link in range(len(LINKS)):
            if not place(link, set()):
                return None
        steps.append(sorted((link, p, d) for (p, d), link in taken.items()))
        have.update({job: t for job in taken})
    return steps


@functools.cache
def schedule():
    return next(s for s in (attempt(seed, 2) for seed in range(1000)) if s is not None)


def place_of_self():
    row, col = lax.axis_index("row"), lax.axis_index("col")
    return (row // 2) % RING, (row // 8) * 2 + col // RING, col % RING, row % 2


def gather_kernel(
    counts_ref, all_ref, stat_ref, own, sums, own_sem, send_sem, recv_sem, twin_send, twin_recv, stat_send, stat_recv
):
    x, y, z, core = place_of_self()

    def device_at(offset, same_core=True):
        px, py, pz = ((me + step) % RING for me, step in zip((x, y, z), offset))
        return ((py // 2) * RING + px) * 2 + (core if same_core else 1 - core), (py % 2) * RING + pz

    twin = device_at((0, 0, 0), False)
    neighbours = [device_at(link) for link in LINKS]
    across = {axis: device_at(tuple(2 * (a == axis) for a in range(3))) for axis in range(3)}

    barrier = pltpu.get_barrier_semaphore()
    peers = [twin, *neighbours, *across.values()]
    for peer in peers:
        pl.semaphore_signal(barrier, inc=1, device_id=peer, device_id_type=MESH)
    counts = counts_ref[...]
    own[...] = counts.astype(jnp.float32).astype(jnp.bfloat16)
    pl.semaphore_wait(barrier, len(peers))

    zero = (0, 0, 0)

    def piece(p, offset):
        if offset == zero:
            return own.at[pl.ds(p * PIECE, PIECE)]
        return all_ref.at[p, number(offset), 0]

    def over_link(link, p, offset):
        n = number(offset)
        return pltpu.make_async_remote_copy(
            src_ref=piece(p, minus(offset, LINKS[link])),
            dst_ref=all_ref.at[p, n, 0],
            send_sem=send_sem.at[p, n],
            recv_sem=recv_sem.at[p, n],
            device_id=neighbours[link],
            device_id_type=MESH,
        )

    def to_twin(p, offset):
        n = number(offset)
        return pltpu.make_async_remote_copy(
            src_ref=piece(p, offset),
            dst_ref=all_ref.at[p, n, 1],
            send_sem=twin_send.at[p, n],
            recv_sem=twin_recv.at[p, n],
            device_id=twin,
            device_id_type=MESH,
        )

    def sum_to(slot, source, target):
        return pltpu.make_async_remote_copy(
            src_ref=sums.at[source],
            dst_ref=sums.at[slot],
            send_sem=stat_send.at[slot],
            recv_sem=stat_recv.at[slot],
            device_id=target,
            device_id_type=MESH,
        )

    def stat_copies(phase):
        if phase == 0:
            return [sum_to(1, 0, twin)]
        axis, base = phase - 1, 4 * phase - 2
        targets = [neighbours[2 * axis], neighbours[2 * axis + 1], across[axis]]
        return [sum_to(base + 1 + i, base, target) for i, target in enumerate(targets)]

    def stat_finish(phase):
        for copy in stat_copies(phase):
            copy.wait()
        if phase == 0:
            sums[2] = sums[0] + sums[1]
        else:
            base = 4 * phase - 2
            sums[base + 4] = (sums[base] + sums[base + 1]) + (sums[base + 2] + sums[base + 3])

    steps = schedule()
    arrived = {(p, zero) for p in range(PARTS)}

    def arrive(link, p, offset):
        if (p, offset) not in arrived:
            arrived.add((p, offset))
            over_link(link, p, offset).wait_recv()
            to_twin(p, offset).start()

    came_by = {(p, offset): link for step in steps for link, p, offset in step}
    for t, step in enumerate(steps):
        for link, p, offset in step:
            source = minus(offset, LINKS[link])
            arrive(came_by.get((p, source)), p, source)
            over_link(link, p, offset).start()
        if t == 1:
            for p in range(PARTS):
                to_twin(p, zero).start()
                pltpu.make_async_copy(piece(p, zero), all_ref.at[p, 0, 0], own_sem.at[p]).start()
            total = jnp.sum(counts, axis=0, keepdims=True)
            square = jnp.sum(counts * counts, axis=0, keepdims=True)
            which = lax.broadcasted_iota(jnp.int32, (8, SNPS), 0)
            sums[0] = jnp.where(which == 0, total, jnp.where(which == 1, square, 0))
            for copy in stat_copies(0):
                copy.start()
        if t in (4, 6, 8, 10):
            phase = (t - 4) // 2
            stat_finish(phase)
            if phase < 3:
                for copy in stat_copies(phase + 1):
                    copy.start()

    total, square = sums[14, 0:1], sums[14, 1:2]
    shifted = total - SAMPLES
    spread = SAMPLES * (square - 2 * total + SAMPLES) - shifted * shifted
    variance = spread.astype(jnp.float32) * (1.0 / (float(SAMPLES) * SAMPLES)) + 1e-05
    mean = total.astype(jnp.float32) * (1.0 / SAMPLES)
    which = lax.broadcasted_iota(jnp.int32, (8, SNPS), 0)
    stat_ref[...] = jnp.where(which == 0, mean, lax.rsqrt(variance))

    for step in steps:
        for link, p, offset in step:
            arrive(link, p, offset)
    for p in range(PARTS):
        pltpu.make_async_copy(piece(p, zero), all_ref.at[p, 0, 0], own_sem.at[p]).wait()
        to_twin(p, zero).wait()
    for step in steps:
        for link, p, offset in step:
            over_link(link, p, offset).wait_send()
            to_twin(p, offset).wait()


def gather(counts):
    slots = (PARTS, len(OFFSETS))
    dma = pltpu.SemaphoreType.DMA
    return pl.pallas_call(
        gather_kernel,
        out_shape=(
            jax.ShapeDtypeStruct((*slots, 2, PIECE, SNPS), jnp.bfloat16),
            jax.ShapeDtypeStruct((8, SNPS), jnp.float32),
        ),
        in_specs=[pl.BlockSpec(memory_space=pltpu.VMEM)],
        out_specs=(pl.BlockSpec(memory_space=pl.ANY), pl.BlockSpec(memory_space=pltpu.VMEM)),
        scratch_shapes=[
            pltpu.VMEM((SHARD, SNPS), jnp.bfloat16),
            pltpu.VMEM((15, 8, SNPS), jnp.int32),
            dma((PARTS,)),
            dma(slots),
            dma(slots),
            dma(slots),
            dma(slots),
            dma((15,)),
            dma((15,)),
        ],
        name="gather_counts",
        compiler_params=pltpu.CompilerParams(
            collective_id=0, has_side_effects=True, vmem_limit_bytes=56 * 2**20
        ),
    )(counts)


def tile_kernel(want_ref, stat_ref, all_ref, out_ref, panels, sem):
    slot, chunk = pl.program_id(0), pl.program_id(1)
    x, y, z, core = place_of_self()
    mean, scale = stat_ref[0:1], stat_ref[1:2]

    def copies(panel, col):
        block = jnp.maximum(want_ref[panel], 0)
        behind = (
            ((x - (block // 2) % RING) % RING) * RING + (y - (block // 8) * 2 - col // RING) % RING
        ) * RING + (z - col % RING) % RING
        other = jnp.where(block % 2 == core, 0, 1)
        return [
            pltpu.make_async_copy(
                all_ref.at[p, behind, other],
                panels.at[panel, pl.ds(col * SHARD + p * PIECE, PIECE)],
                sem.at[panel, col, p],
            )
            for p in range(PARTS)
        ]

    def fetch(panel):
        def one(col, carry):
            for copy in copies(panel, col):
                copy.start()
            return carry

        lax.fori_loop(0, COL_COUNT, one, 0)

    def standardize(panel, col):
        for copy in copies(panel, col):
            copy.wait()
        rows = pl.ds(col * SHARD, SHARD)
        counts = panels[panel, rows].astype(jnp.float32)
        panels[panel, rows] = ((counts - mean) * scale).astype(jnp.bfloat16)

    def live(which):
        return want_ref[2 * which] >= 0

    @pl.when((slot == 0) & (chunk == 0))
    def _():
        for which in range(2):

            @pl.when(live(which))
            def _():
                fetch(2 * which + 1)
                fetch(2 * which)

    @pl.when((slot == 0) & (chunk == 0) & live(0))
    def _():
        lax.fori_loop(0, COL_COUNT, lambda col, c: (standardize(1, col), c)[1], 0)

    @pl.when((slot == 0) & live(1))
    def _():
        standardize(3, chunk)

    @pl.when(live(slot))
    def _():
        standardize(2 * slot, chunk)
        left = panels[2 * slot, pl.ds(chunk * CHUNK, CHUNK)]
        product = lax.dot_general(
            left, panels[2 * slot + 1], (((1,), (1,)), ((), ())), preferred_element_type=jnp.float32
        )
        out_ref[0, 0] = (product * (1.0 / SNPS)).astype(jnp.bfloat16)

    @pl.when(jnp.logical_not(live(slot)))
    def _():
        out_ref[0, 0] = jnp.zeros((CHUNK, BLOCK), jnp.bfloat16)


def tiles(want, stats, everything):
    return pl.pallas_call(
        tile_kernel,
        out_shape=jax.ShapeDtypeStruct((1, 2, BLOCK, BLOCK), jnp.bfloat16),
        grid_spec=pltpu.PrefetchScalarGridSpec(
            num_scalar_prefetch=1,
            grid=(2, BLOCK // CHUNK),
            in_specs=[
                pl.BlockSpec((8, SNPS), lambda s, i, w: (0, 0)),
                pl.BlockSpec(memory_space=pl.ANY),
            ],
            out_specs=pl.BlockSpec((1, 1, CHUNK, BLOCK), lambda s, i, w: (0, s, i, 0)),
            scratch_shapes=[
                pltpu.VMEM((4, BLOCK, SNPS), jnp.bfloat16),
                pltpu.SemaphoreType.DMA((4, COL_COUNT, PARTS)),
            ],
        ),
        name="tile_products",
        compiler_params=pltpu.CompilerParams(vmem_limit_bytes=48 * 2**20),
    )(want, stats, everything)


def on_device(genotypes, pairs):
    everything, stats = gather(genotypes)
    device = lax.axis_index("row") * COL_COUNT + lax.axis_index("col")
    want = lax.dynamic_index_in_dim(pairs, device, 0, keepdims=False).reshape(4)
    return tiles(want, stats, everything)


def solution(mesh):
    return jax.shard_map(
        on_device,
        mesh=mesh,
        in_specs=(P(("row", "col"), None), P()),
        out_specs=P(("row", "col"), None, None, None),
        check_vma=False,
    )
```

```python
import jax
import jax.numpy as jnp
import numpy as np
from jax import lax
from jax.experimental import pallas as pl
from jax.experimental.pallas import tpu as pltpu
from jax.sharding import PartitionSpec as P

MESH = pl.DeviceIdType.MESH
SNPS = 512
RING = 4
ROW_COUNT = 16
COL_COUNT = 8
SHARD = 256
SAMPLES = SHARD * ROW_COUNT * COL_COUNT
BLOCK = SHARD * COL_COUNT
STREAMS = 2
PARTS = 2
PIECE = SHARD // (STREAMS * PARTS)
PANELS = 4
LINKS = ((1, 0, 0), (3, 0, 0), (0, 1, 0), (0, 3, 0), (0, 0, 1), (0, 0, 3))
PER_LINK = 2
CHUNK = 512

RELAYS = (
    ((1, 16), (0, 48), (0, 4), (1, 12), (0, 1), (0, 3)),
    ((0, 20), (0, 32), (0, 8), (0, 15), (1, 13), (1, 3)),
    ((0, 24), (0, 56), (1, 7), (0, 44), (0, 21), (0, 14)),
    ((0, 30), (1, 61), (1, 20), (0, 10), (0, 22), (0, 47)),
    ((0, 38), (1, 45), (0, 18), (1, 57), (0, 57), (1, 6)),
    ((1, 19), (1, 51), (1, 10), (1, 41), (0, 39), (0, 46)),
    ((1, 35), (0, 49), (1, 55), (1, 31), (1, 42), (0, 29)),
)
DIRECT = (
    ((0, 9), (0, 19), (0, 34), (0, 40), (0, 45), (0, 54), (0, 55), (0, 62), (0, 63), (1, 9), (1, 22), (1, 26), (1, 29), (1, 36)),
    ((0, 6), (0, 16), (0, 23), (0, 28), (0, 33), (0, 41), (1, 4), (1, 15), (1, 25), (1, 39), (1, 48), (1, 54), (1, 58), (1, 60)),
    ((0, 7), (0, 26), (0, 35), (0, 42), (0, 43), (0, 53), (0, 61), (1, 1), (1, 24), (1, 33), (1, 49), (1, 59)),
    ((0, 12), (0, 17), (0, 52), (0, 60), (1, 2), (1, 8), (1, 27), (1, 28), (1, 37), (1, 38), (1, 47), (1, 53), (1, 63)),
    ((0, 5), (0, 25), (0, 31), (0, 36), (0, 50), (0, 58), (1, 11), (1, 14), (1, 17), (1, 21), (1, 32), (1, 43), (1, 46), (1, 52), (1, 62)),
    ((0, 2), (0, 11), (0, 13), (0, 27), (0, 37), (0, 51), (0, 59), (1, 5), (1, 18), (1, 23), (1, 30), (1, 34), (1, 40), (1, 44), (1, 50), (1, 56)),
)

def offset_of(n):
    return n // (RING * RING), n // RING % RING, n % RING


def number(offset):
    return (offset[0] * RING + offset[1]) * RING + offset[2]


def before(n, link):
    return number(tuple((i - j) % RING for i, j in zip(offset_of(n), LINKS[link])))


HELD = tuple((p, 0) for p in range(PARTS)) + tuple(item for step in RELAYS for item in step)
SLOT_OF = {item: i for i, item in enumerate(HELD)}
CAME_BY = {item: link for step in RELAYS for link, item in enumerate(step)}


def class_of(n, y_lo):
    dx, dy, _ = offset_of(n)
    return (dx * 2 + y_lo) * 2 + ((dy + 1 - y_lo) // 2) % 2


def tables():
    lists = {}
    for y_lo in range(2):
        for c in range(RING):
            for half in range(2):
                kind = (c * 2 + y_lo) * 2 + half
                links = [
                    [(SLOT_OF[p, before(n, e)], p, n) for p, n in DIRECT[e] if class_of(n, y_lo) == kind]
                    for e in range(len(LINKS))
                ]
                own = [(i, p, n) for i, (p, n) in enumerate(HELD) if class_of(n, y_lo) == kind]
                lists[kind] = (links, own)
    assert all(len(part) <= PER_LINK for links, _ in lists.values() for part in links)
    own_most = max(len(own) for _, own in lists.values())
    pieces = len(LINKS) * PER_LINK + own_most
    slots = np.zeros((len(lists), pieces), np.int32)
    items = np.full((len(lists), pieces), -1, np.int32)
    for kind, (links, own) in lists.items():
        for base, part in [(e * PER_LINK, part) for e, part in enumerate(links)] + [(len(links) * PER_LINK, own)]:
            for i, (slot, p, n) in enumerate(part):
                slots[kind, base + i] = slot
                items[kind, base + i] = p * RING**3 + n
    return slots, items, own_most


SLOTS, ITEMS, OWN = tables()
FROM_LINKS = len(LINKS) * PER_LINK
PIECES = FROM_LINKS + OWN


def place_of_self():
    row, col = lax.axis_index("row"), lax.axis_index("col")
    return (row // 2) % RING, (row // 8) * 2 + col // RING, col % RING, row % 2


def kind_of(block, x, y):
    behind = (x - lax.shift_right_logical(block, 1)) & (RING - 1)
    half = ((y // 2) - lax.shift_right_logical(block, 3)) & 1
    return (behind * 2 + y % 2) * 2 + half


def gather_kernel(
    counts_ref, pairs_ref, slots_ref, out_ref,
    held, sums, away, near,
    twin_send, twin_recv, relay_send, relay_recv, stat_send, stat_recv,
    link_send, link_recv, near_send, near_recv, own_sem,
):
    x, y, z, core = place_of_self()

    def place(offset):
        return tuple((me + step) % RING for me, step in zip((x, y, z), offset))

    def device_at(offset, on_core):
        px, py, pz = place(offset)
        return ((py // 2) * RING + px) * 2 + on_core, (py % 2) * RING + pz

    twin = device_at((0, 0, 0), 1 - core)
    neighbours = [device_at(link, core) for link in LINKS]
    across = [device_at(tuple(2 * (a == axis) for a in range(3)), core) for axis in range(3)]
    others = [device_at(link, 1 - core) for link in LINKS]

    barrier = pltpu.get_barrier_semaphore()
    peers = [twin, *neighbours, *others, *across]
    for peer in peers:
        pl.semaphore_signal(barrier, inc=1, device_id=peer, device_id_type=MESH)

    def as_bf16(first, rows):
        return counts_ref[pl.ds(first, rows)].astype(jnp.float32).astype(jnp.bfloat16)

    mine, theirs = core * (SHARD // 2), (1 - core) * (SHARD // 2)
    for p in range(PARTS):
        near[0, p] = as_bf16(pl.multiple_of(theirs + p * PIECE, PIECE), PIECE)
        held[p, core] = as_bf16(pl.multiple_of(mine + p * PIECE, PIECE), PIECE)
    pl.semaphore_wait(barrier, len(peers))

    def swap(p):
        return pltpu.make_async_remote_copy(
            src_ref=near.at[0, p],
            dst_ref=held.at[p, core],
            send_sem=twin_send.at[p],
            recv_sem=twin_recv.at[p],
            device_id=twin,
            device_id_type=MESH,
        )

    def swapped(p):
        return pltpu.make_async_remote_copy(
            src_ref=near.at[0, p],
            dst_ref=held.at[p, 1 - core],
            send_sem=twin_send.at[p],
            recv_sem=twin_recv.at[p],
            device_id=twin,
            device_id_type=MESH,
        )

    for p in range(PARTS):
        swap(p).start()

    def sum_to(slot, source, target):
        return pltpu.make_async_remote_copy(
            src_ref=sums.at[source],
            dst_ref=sums.at[slot],
            send_sem=stat_send.at[slot],
            recv_sem=stat_recv.at[slot],
            device_id=target,
            device_id_type=MESH,
        )

    def stat_copies(phase):
        if phase == 0:
            return [sum_to(1, 0, twin)]
        axis, base = phase - 1, 4 * phase - 2
        targets = [neighbours[2 * axis], neighbours[2 * axis + 1], across[axis]]
        return [sum_to(base + 1 + i, base, target) for i, target in enumerate(targets)]

    def stat_finish(phase):
        for copy in stat_copies(phase):
            copy.wait()
        if phase == 0:
            sums[2] = sums[0] + sums[1]
        else:
            base = 4 * phase - 2
            sums[base + 4] = (sums[base] + sums[base + 1]) + (sums[base + 2] + sums[base + 3])

    def stat_start():
        counts = counts_ref[...]
        total = jnp.sum(counts, axis=0, keepdims=True)
        square = jnp.sum(counts * counts, axis=0, keepdims=True)
        which = lax.broadcasted_iota(jnp.int32, (8, SNPS), 0)
        sums[0] = jnp.where(which == 0, total, jnp.where(which == 1, square, 0))
        for copy in stat_copies(0):
            copy.start()

    def relay(item, half):
        slot, link = SLOT_OF[item], CAME_BY[item]
        source = SLOT_OF[item[0], before(item[1], link)]
        return pltpu.make_async_remote_copy(
            src_ref=held.at[source, half],
            dst_ref=held.at[slot, half],
            send_sem=relay_send.at[slot, half],
            recv_sem=relay_recv.at[slot, half],
            device_id=neighbours[link],
            device_id_type=MESH,
        )

    arrived = set()

    def arrive(item, half):
        if (item, half) not in arrived:
            arrived.add((item, half))
            relay(item, half).wait_recv()

    for p in range(PARTS):
        swap(p).wait_send()
        swapped(p).wait_recv()
        arrived.update(((p, 0), half) for half in range(2))
    for t, step in enumerate(RELAYS):
        for half in range(2):
            for link, item in enumerate(step):
                arrive((item[0], before(item[1], link)), half)
                relay(item, half).start()
            if t == 0 and half == 0:
                stat_start()
        if 0 < t < 5:
            stat_finish(t - 1)
            if t < 4:
                for copy in stat_copies(t):
                    copy.start()
    for step in RELAYS:
        for half in range(2):
            for item in step:
                arrive(item, half)

    total, square = sums[14, 0:1], sums[14, 1:2]
    shifted = total - SAMPLES
    spread = SAMPLES * (square - 2 * total + SAMPLES) - shifted * shifted
    variance = spread.astype(jnp.float32) * (1.0 / (float(SAMPLES) * SAMPLES)) + 1e-05
    mean = total.astype(jnp.float32) * (1.0 / SAMPLES)
    scale = lax.rsqrt(variance)

    def standard(slot, half, factor):
        return ((held[slot, half].astype(jnp.float32) - mean) * (scale * factor)).astype(jnp.bfloat16)

    def wanted(device, panel):
        return jnp.maximum(pairs_ref[panel, device[0] * COL_COUNT + device[1]], 0)

    def to_link(link, to_core, panel):
        return pltpu.make_async_remote_copy(
            src_ref=away.at[link, to_core, panel],
            dst_ref=out_ref.at[panel, core, pl.ds(link * PER_LINK, PER_LINK)],
            send_sem=link_send.at[link, to_core, panel],
            recv_sem=link_recv.at[link, core, panel],
            device_id=device_at(LINKS[link], to_core),
            device_id_type=MESH,
        )

    def from_link(link, stream, panel):
        return pltpu.make_async_remote_copy(
            src_ref=away.at[link, 0, panel],
            dst_ref=out_ref.at[panel, stream, pl.ds(link * PER_LINK, PER_LINK)],
            send_sem=link_send.at[link, 0, panel],
            recv_sem=link_recv.at[link, stream, panel],
            device_id=neighbours[link],
            device_id_type=MESH,
        )

    def to_twin(panel, stream):
        return pltpu.make_async_remote_copy(
            src_ref=near.at[1 + panel, pl.ds(0, OWN)],
            dst_ref=out_ref.at[panel, stream, pl.ds(FROM_LINKS, OWN)],
            send_sem=near_send.at[panel],
            recv_sem=near_recv.at[panel],
            device_id=twin,
            device_id_type=MESH,
        )

    def to_self(panel):
        return pltpu.make_async_copy(
            near.at[1 + PANELS + panel, pl.ds(0, OWN)],
            out_ref.at[panel, core, pl.ds(FROM_LINKS, OWN)],
            own_sem.at[panel],
        )

    def send_panel(panel, carry):
        factor = jnp.where(panel % 2 == 0, 1.0 / SNPS, 1.0).astype(jnp.float32)
        for to_core in range(2):
            for link, step in enumerate(LINKS):
                block = wanted(device_at(step, to_core), panel)
                px, py, _ = place(step)
                kind = kind_of(block, px, py)
                for i in range(PER_LINK):
                    slot = slots_ref[kind, link * PER_LINK + i]
                    away[link, to_core, panel, i] = standard(slot, block & 1, factor)
                to_link(link, to_core, panel).start()
        for which, device in enumerate((twin, device_at((0, 0, 0), core))):
            block = wanted(device, panel)
            kind = kind_of(block, x, y)

            def one(i, c):
                slot = slots_ref[kind, FROM_LINKS + i]
                near[1 + which * PANELS + panel, i] = standard(slot, block & 1, factor)
                return c

            lax.fori_loop(0, OWN, one, 0)
            if which == 0:
                to_twin(panel, core).start()
            else:
                to_self(panel).start()
        return carry

    lax.fori_loop(0, PANELS, send_panel, 0)

    def finish_panel(panel, carry):
        for half in range(2):
            for link in range(len(LINKS)):
                to_link(link, half, panel).wait_send()
                from_link(link, half, panel).wait_recv()
        to_twin(panel, core).wait_send()
        to_twin(panel, 1 - core).wait_recv()
        to_self(panel).wait()
        return carry

    for step in RELAYS:
        for half in range(2):
            for item in step:
                relay(item, half).wait_send()
    lax.fori_loop(0, PANELS, finish_panel, 0)


def gather(counts, pairs):
    dma = pltpu.SemaphoreType.DMA
    return pl.pallas_call(
        gather_kernel,
        out_shape=jax.ShapeDtypeStruct((PANELS, STREAMS, PIECES, PIECE, SNPS), jnp.bfloat16),
        in_specs=[
            pl.BlockSpec(memory_space=pltpu.VMEM),
            pl.BlockSpec(memory_space=pltpu.SMEM),
            pl.BlockSpec(memory_space=pltpu.SMEM),
        ],
        out_specs=pl.BlockSpec(memory_space=pl.ANY),
        scratch_shapes=[
            pltpu.VMEM((len(HELD), 2, PIECE, SNPS), jnp.bfloat16),
            pltpu.VMEM((15, 8, SNPS), jnp.int32),
            pltpu.VMEM((len(LINKS), 2, PANELS, PER_LINK, PIECE, SNPS), jnp.bfloat16),
            pltpu.VMEM((1 + 2 * PANELS, max(OWN, PARTS), PIECE, SNPS), jnp.bfloat16),
            dma((PARTS,)),
            dma((PARTS,)),
            dma((len(HELD), 2)),
            dma((len(HELD), 2)),
            dma((15,)),
            dma((15,)),
            dma((len(LINKS), 2, PANELS)),
            dma((len(LINKS), 2, PANELS)),
            dma((PANELS,)),
            dma((PANELS,)),
            dma((PANELS,)),
        ],
        name="gather_panels",
        compiler_params=pltpu.CompilerParams(
            collective_id=0, has_side_effects=True, vmem_limit_bytes=56 * 2**20
        ),
    )(counts, pairs, jnp.asarray(SLOTS))


def tile_kernel(pairs_ref, items_ref, all_ref, out_ref, panels, sem):
    slot, chunk = pl.program_id(0), pl.program_id(1)
    x, y, z, core = place_of_self()
    device = lax.axis_index("row") * COL_COUNT + lax.axis_index("col")

    def fetch(panel):
        block = jnp.maximum(pairs_ref[panel, device], 0)
        kind = kind_of(block, x, y)

        def one(i, carry):
            item = items_ref[kind, i]

            @pl.when(item >= 0)
            def _():
                oy = (y - (item // RING)) & (RING - 1)
                oz = (z - item) & (RING - 1)
                first = ((oy & 1) * RING + oz) * SHARD + (item // RING**3) * PIECE
                for stream in range(STREAMS):
                    rows = pl.ds(pl.multiple_of(first + stream * (SHARD // 2), PIECE), PIECE)
                    pltpu.make_async_copy(all_ref.at[panel, stream, i], panels.at[panel, rows], sem.at[panel]).start()

            return carry

        lax.fori_loop(0, PIECES, one, 0)

    def arrive(panel):
        pltpu.make_async_copy(panels.at[panel], panels.at[panel], sem.at[panel]).wait()

    def live(which):
        return pairs_ref[2 * which, device] >= 0

    @pl.when((slot == 0) & (chunk == 0))
    def _():
        for which in range(2):

            @pl.when(live(which))
            def _():
                fetch(2 * which + 1)
                fetch(2 * which)

    @pl.when(live(slot))
    def _():
        @pl.when(chunk == 0)
        def _():
            arrive(2 * slot)
            arrive(2 * slot + 1)

        left = panels[2 * slot, pl.ds(pl.multiple_of(chunk * CHUNK, CHUNK), CHUNK)]
        product = lax.dot_general(
            left, panels[2 * slot + 1], (((1,), (1,)), ((), ())), preferred_element_type=jnp.float32
        )
        out_ref[0, 0] = product.astype(jnp.bfloat16)

    @pl.when(jnp.logical_not(live(slot)))
    def _():
        out_ref[0, 0] = jnp.zeros((CHUNK, BLOCK), jnp.bfloat16)


def tiles(pairs, panels):
    return pl.pallas_call(
        tile_kernel,
        out_shape=jax.ShapeDtypeStruct((1, 2, BLOCK, BLOCK), jnp.bfloat16),
        grid_spec=pltpu.PrefetchScalarGridSpec(
            num_scalar_prefetch=2,
            grid=(2, BLOCK // CHUNK),
            in_specs=[pl.BlockSpec(memory_space=pl.ANY)],
            out_specs=pl.BlockSpec((1, 1, CHUNK, BLOCK), lambda s, i, *_: (0, s, i, 0)),
            scratch_shapes=[
                pltpu.VMEM((PANELS, BLOCK, SNPS), jnp.bfloat16),
                pltpu.SemaphoreType.DMA((PANELS,)),
            ],
        ),
        name="tile_products",
        compiler_params=pltpu.CompilerParams(vmem_limit_bytes=48 * 2**20),
    )(pairs, jnp.asarray(ITEMS), panels)


def on_device(genotypes, pairs):
    by_panel = pairs.transpose(1, 2, 0).reshape(PANELS, -1)
    return tiles(by_panel, gather(genotypes, by_panel))


def solution(mesh):
    return jax.shard_map(
        on_device,
        mesh=mesh,
        in_specs=(P(("row", "col"), None), P()),
        out_specs=P(("row", "col"), None, None, None),
        check_vma=False,
    )
```

```python
import jax
import jax.numpy as jnp
import numpy as np
from jax import lax
from jax.experimental import pallas as pl
from jax.experimental.pallas import tpu as pltpu
from jax.sharding import PartitionSpec as P

MESH = pl.DeviceIdType.MESH
SNPS = 512
RING = 4
ROW_COUNT = 16
COL_COUNT = 8
SHARD = 256
SAMPLES = SHARD * ROW_COUNT * COL_COUNT
BLOCK = SHARD * COL_COUNT
STREAMS = 2
PARTS = 2
PIECE = SHARD // (STREAMS * PARTS)
PANELS = 4
LINKS = ((1, 0, 0), (3, 0, 0), (0, 1, 0), (0, 3, 0), (0, 0, 1), (0, 0, 3))
PER_LINK = 2
CHUNK = 512

RELAYS = (
    ((0, 16), (0, 48), (1, 4), (1, 12), (1, 1), (0, 3)),
    ((0, 32), (1, 48), (0, 4), (0, 60), (1, 2), (0, 19)),
    ((1, 17), (1, 52), (0, 20), (0, 15), (1, 13), (1, 15)),
    ((1, 31), (1, 36), (0, 24), (1, 9), (0, 61), (0, 23)),
    ((0, 39), (0, 63), (1, 6), (0, 44), (0, 25), (1, 55)),
    ((1, 47), (0, 45), (0, 49), (1, 27), (1, 37), (0, 22)),
    ((0, 38), (0, 6), (1, 59), (0, 59), (0, 46), (1, 46)),
)
DIRECT = (
    ((0, 1), (0, 13), (0, 40), (0, 41), (0, 54), (0, 62), (1, 11), (1, 18), (1, 22), (1, 25), (1, 29), (1, 33), (1, 53), (1, 62)),
    ((0, 8), (0, 9), (0, 30), (0, 33), (0, 43), (1, 20), (1, 21), (1, 30), (1, 32), (1, 43), (1, 50), (1, 54), (1, 57), (1, 61)),
    ((0, 10), (0, 26), (0, 29), (0, 52), (0, 53), (1, 3), (1, 10), (1, 19), (1, 34), (1, 35), (1, 40), (1, 41), (1, 63)),
    ((0, 2), (0, 11), (0, 28), (0, 31), (0, 34), (0, 35), (0, 42), (0, 55), (0, 57), (1, 8), (1, 23), (1, 42), (1, 51), (1, 60)),
    ((0, 5), (0, 12), (0, 17), (0, 21), (0, 36), (0, 50), (0, 56), (1, 5), (1, 14), (1, 24), (1, 28), (1, 38), (1, 44), (1, 49), (1, 56)),
    ((0, 7), (0, 14), (0, 18), (0, 27), (0, 37), (0, 47), (0, 51), (0, 58), (1, 7), (1, 16), (1, 26), (1, 39), (1, 45), (1, 58)),
)

def offset_of(n):
    return n // (RING * RING), n // RING % RING, n % RING


def number(offset):
    return (offset[0] * RING + offset[1]) * RING + offset[2]


def before(n, link):
    return number(tuple((i - j) % RING for i, j in zip(offset_of(n), LINKS[link])))


HELD = tuple((p, 0) for p in range(PARTS)) + tuple(item for step in RELAYS for item in step)
LANES = 128
SLOT_OF = {item: i for i, item in enumerate(HELD)}
CAME_BY = {item: link for step in RELAYS for link, item in enumerate(step)}


def class_of(n, y_lo):
    dx, dy, _ = offset_of(n)
    return (dx * 2 + y_lo) * 2 + ((dy + 1 - y_lo) // 2) % 2


def tables():
    table = np.zeros((18, LANES), np.int32)
    own_most = 0
    for y_lo in range(2):
        for kind in sorted({class_of(n, y_lo) for n in range(RING**3)}):
            places = []
            for e, items in enumerate(DIRECT):
                mine = [(p, n) for p, n in items if class_of(n, y_lo) == kind]
                assert len(mine) <= PER_LINK
                places += [(e * PER_LINK + i, SLOT_OF[p, before(n, e)], p, n) for i, (p, n) in enumerate(mine)]
            own = [(slot, p, n) for slot, (p, n) in enumerate(HELD) if class_of(n, y_lo) == kind]
            own_most = max(own_most, len(own))
            places += [(FROM_LINKS + i, *one) for i, one in enumerate(own)]
            assert len(places) == PARTS * COL_COUNT
            for place, slot, p, n in places:
                table[kind, place] = slot
                table[16 + y_lo, p * RING**3 + n] = place
    return table, own_most


FROM_LINKS = len(LINKS) * PER_LINK
TABLE, OWN = tables()
PIECES = FROM_LINKS + OWN


def place_of_self():
    row, col = lax.axis_index("row"), lax.axis_index("col")
    return (row // 2) % RING, (row // 8) * 2 + col // RING, col % RING, row % 2


def kind_of(block, x, y):
    behind = (x - lax.shift_right_logical(block, 1)) & (RING - 1)
    half = ((y // 2) - lax.shift_right_logical(block, 3)) & 1
    return (behind * 2 + y % 2) * 2 + half


def gather_kernel(
    counts_hbm, pairs_hbm, table_hbm, tile_ref, panels_ref,
    counts_ref, pairs_ref, table_ref, held, sums, away, near, landed0, landed1, landed2, landed3, left, right,
    load_sem, twin_send, twin_recv, relay_send, relay_recv, stat_send, stat_recv,
    link_send, link_recv, near_send, near_recv,
):
    x, y, z, core = place_of_self()
    landed = (landed0, landed1, landed2, landed3)

    def place(offset):
        return tuple((me + step) % RING for me, step in zip((x, y, z), offset))

    def device_at(offset, on_core):
        px, py, pz = place(offset)
        return ((py // 2) * RING + px) * 2 + on_core, (py % 2) * RING + pz

    here = (0, 0, 0)
    twin = device_at(here, 1 - core)
    neighbours = [device_at(link, core) for link in LINKS]
    across = [device_at(tuple(2 * (a == axis) for a in range(3)), core) for axis in range(3)]
    others = [device_at(link, 1 - core) for link in LINKS]

    barrier = pltpu.get_barrier_semaphore()
    peers = [twin, *neighbours, *others, *across]
    for peer in peers:
        pl.semaphore_signal(barrier, inc=1, device_id=peer, device_id_type=MESH)
    loads = [
        pltpu.make_async_copy(source, target, load_sem.at[i])
        for i, (source, target) in enumerate(
            ((counts_hbm, counts_ref), (pairs_hbm, pairs_ref), (table_hbm, table_ref))
        )
    ]
    for load in loads:
        load.start()
    loads[0].wait()

    def as_bf16(first, rows):
        return counts_ref[pl.ds(first, rows)].astype(jnp.float32).astype(jnp.bfloat16)

    mine, theirs = core * (SHARD // 2), (1 - core) * (SHARD // 2)
    for p in range(PARTS):
        near[2, p] = as_bf16(pl.multiple_of(theirs + p * PIECE, PIECE), PIECE)
        held[p, core] = as_bf16(pl.multiple_of(mine + p * PIECE, PIECE), PIECE)
    halves = (core, 1 - core)

    def swap(p, half):
        return pltpu.make_async_remote_copy(
            src_ref=near.at[2, p],
            dst_ref=held.at[p, half],
            send_sem=twin_send.at[p],
            recv_sem=twin_recv.at[p],
            device_id=twin,
            device_id_type=MESH,
        )

    pl.semaphore_wait(barrier, len(peers))
    for p in range(PARTS):
        swap(p, core).start()

    def sum_to(slot, source, target):
        return pltpu.make_async_remote_copy(
            src_ref=sums.at[source],
            dst_ref=sums.at[slot],
            send_sem=stat_send.at[slot],
            recv_sem=stat_recv.at[slot],
            device_id=target,
            device_id_type=MESH,
        )

    def stat_copies(phase):
        if phase == 0:
            return [sum_to(1, 0, twin)]
        axis, base = phase - 1, 4 * phase - 2
        targets = [neighbours[2 * axis], neighbours[2 * axis + 1], across[axis]]
        return [sum_to(base + 1 + i, base, target) for i, target in enumerate(targets)]

    def stat_finish(phase):
        for copy in stat_copies(phase):
            copy.wait()
        if phase == 0:
            sums[2] = sums[0] + sums[1]
        else:
            base = 4 * phase - 2
            sums[base + 4] = (sums[base] + sums[base + 1]) + (sums[base + 2] + sums[base + 3])

    def stat_start():
        counts = counts_ref[...]
        total = jnp.sum(counts, axis=0, keepdims=True)
        square = jnp.sum(counts * counts, axis=0, keepdims=True)
        which = lax.broadcasted_iota(jnp.int32, (8, SNPS), 0)
        sums[0] = jnp.where(which == 0, total, jnp.where(which == 1, square, 0))
        for copy in stat_copies(0):
            copy.start()

    def relay(item, half):
        slot, link = SLOT_OF[item], CAME_BY[item]
        source = SLOT_OF[item[0], before(item[1], link)]
        return pltpu.make_async_remote_copy(
            src_ref=held.at[source, halves[half]],
            dst_ref=held.at[slot, halves[half]],
            send_sem=relay_send.at[slot, half],
            recv_sem=relay_recv.at[slot, half],
            device_id=neighbours[link],
            device_id_type=MESH,
        )

    arrived = {((p, 0), 0) for p in range(PARTS)}

    def arrive(item, half):
        if (item, half) not in arrived:
            arrived.add((item, half))
            if item[1] == 0:
                swap(item[0], halves[1]).wait_recv()
            else:
                relay(item, half).wait_recv()

    for t, step in enumerate(RELAYS):
        for half in range(2):
            for link, item in enumerate(step):
                arrive((item[0], before(item[1], link)), half)
                relay(item, half).start()
            if t == 0 and half == 0:
                stat_start()
        if 0 < t < 5:
            stat_finish(t - 1)
            if t < 4:
                for copy in stat_copies(t):
                    copy.start()
    for step in RELAYS:
        for half in range(2):
            for item in step:
                arrive(item, half)
    loads[1].wait()
    loads[2].wait()

    total, square = sums[14, 0:1], sums[14, 1:2]
    shifted = total - SAMPLES
    spread = SAMPLES * (square - 2 * total + SAMPLES) - shifted * shifted
    variance = spread.astype(jnp.float32) * (1.0 / (float(SAMPLES) * SAMPLES)) + 1e-05
    mean = total.astype(jnp.float32) * (1.0 / SAMPLES)
    scale = lax.rsqrt(variance)

    def standard(slot, half, factor):
        return ((held[slot, half].astype(jnp.float32) - mean) * (scale * factor)).astype(jnp.bfloat16)

    def wanted(device, panel):
        return jnp.maximum(pairs_ref[panel, device[0] * COL_COUNT + device[1]], 0)

    def step_of(link):
        step = 1 + 2 * (link % 2)
        return tuple(jnp.where(link // 2 == axis, step, 0) for axis in range(3))

    def to_link(link, to_core, panel, stream):
        return pltpu.make_async_remote_copy(
            src_ref=away.at[link, to_core, panel % 2],
            dst_ref=landed[panel].at[stream, pl.ds(link * PER_LINK, PER_LINK)],
            send_sem=link_send.at[link, to_core, panel],
            recv_sem=link_recv.at[link, stream, panel],
            device_id=device_at(step_of(link), to_core),
            device_id_type=MESH,
        )

    def to_twin(panel, stream):
        return pltpu.make_async_remote_copy(
            src_ref=near.at[panel % 2],
            dst_ref=landed[panel].at[stream, pl.ds(FROM_LINKS, OWN)],
            send_sem=near_send.at[panel],
            recv_sem=near_recv.at[panel],
            device_id=twin,
            device_id_type=MESH,
        )

    def sent(panel):
        for link in range(len(LINKS)):
            for to_core in range(2):
                to_link(link, to_core, panel, core).wait_send()
        to_twin(panel, core).wait_send()

    def send_panel(panel):
        if panel >= 2:
            sent(panel - 2)
        factor = 1.0 / SNPS if panel % 2 == 0 else 1.0

        def message(m, carry):
            to_core, link = m // len(LINKS), m % len(LINKS)
            step = step_of(link)
            block = wanted(device_at(step, to_core), panel)
            px, py, _ = place(step)
            kind = kind_of(block, px, py)
            for i in range(PER_LINK):
                slot = table_ref[kind, link * PER_LINK + i]
                away[link, to_core, panel % 2, i] = standard(slot, block & 1, factor)
            to_link(link, to_core, panel, core).start()
            return carry

        lax.fori_loop(0, 2 * len(LINKS), message, 0)
        for device in (twin, device_at(here, core)):
            block = wanted(device, panel)
            kind = kind_of(block, x, y)

            def one(i, carry):
                piece = standard(table_ref[kind, FROM_LINKS + i], block & 1, factor)
                if device is twin:
                    near[panel % 2, i] = piece
                else:
                    landed[panel][core, FROM_LINKS + i] = piece
                return carry

            lax.fori_loop(0, OWN, one, 0)
            if device is twin:
                to_twin(panel, core).start()

    for panel in range(PANELS):
        send_panel(panel)

    def in_order(panel, target):
        for link in range(len(LINKS)):
            for stream in range(STREAMS):
                to_link(link, 0, panel, stream).wait_recv()
        to_twin(panel, 1 - core).wait_recv()
        block = wanted(device_at(here, core), panel)
        live = pairs_ref[panel, device_at(here, core)[0] * COL_COUNT + device_at(here, core)[1]] >= 0
        keep = jnp.where(live, 1.0, 0.0).astype(jnp.bfloat16)
        dx = (x - lax.shift_right_logical(block, 1)) & (RING - 1)

        def one(col, carry):
            dy = (y - (2 * lax.shift_right_logical(block, 3) + col // RING)) & (RING - 1)
            dz = (z - col % RING) & (RING - 1)
            for p in range(PARTS):
                place = table_ref[16 + y % 2, p * RING**3 + (dx * RING + dy) * RING + dz]
                for stream in range(STREAMS):
                    first = col * SHARD + stream * (SHARD // 2) + p * PIECE
                    rows = pl.ds(pl.multiple_of(first, PIECE), PIECE)
                    target[rows] = landed[panel][stream, place] * keep
            return carry

        lax.fori_loop(0, COL_COUNT, one, 0)

    in_order(0, left)
    in_order(1, right)

    def multiply(i, carry):
        rows = pl.ds(pl.multiple_of(i * CHUNK, CHUNK), CHUNK)
        product = lax.dot_general(
            left[rows], right[...], (((1,), (1,)), ((), ())), preferred_element_type=jnp.float32
        )
        tile_ref[rows] = product.astype(jnp.bfloat16)
        return carry

    lax.fori_loop(0, BLOCK // CHUNK, multiply, 0)
    in_order(2, panels_ref.at[0])
    in_order(3, panels_ref.at[1])
    for panel in (2, 3):
        sent(panel)
    for p in range(PARTS):
        swap(p, core).wait_send()
    for step in RELAYS:
        for half in range(2):
            for item in step:
                relay(item, half).wait_send()


def gather(counts, pairs):
    dma = pltpu.SemaphoreType.DMA
    bf16 = jnp.bfloat16
    return pl.pallas_call(
        gather_kernel,
        out_shape=(
            jax.ShapeDtypeStruct((BLOCK, BLOCK), bf16),
            jax.ShapeDtypeStruct((2, BLOCK, SNPS), bf16),
        ),
        in_specs=[pl.BlockSpec(memory_space=pltpu.HBM)] * 3,
        out_specs=(pl.BlockSpec(memory_space=pltpu.VMEM),) * 2,
        scratch_shapes=[
            pltpu.VMEM((SHARD, SNPS), jnp.int32),
            pltpu.SMEM((PANELS, LANES), jnp.int32),
            pltpu.SMEM(TABLE.shape, jnp.int32),
            pltpu.VMEM((len(HELD), 2, PIECE, SNPS), bf16),
            pltpu.VMEM((15, 8, SNPS), jnp.int32),
            pltpu.VMEM((len(LINKS), 2, 2, PER_LINK, PIECE, SNPS), bf16),
            pltpu.VMEM((3, OWN, PIECE, SNPS), bf16),
            *[pltpu.VMEM((STREAMS, PIECES, PIECE, SNPS), bf16) for _ in range(PANELS)],
            pltpu.VMEM((BLOCK, SNPS), bf16),
            pltpu.VMEM((BLOCK, SNPS), bf16),
            dma((3,)),
            dma((PARTS,)),
            dma((PARTS,)),
            dma((len(HELD), 2)),
            dma((len(HELD), 2)),
            dma((15,)),
            dma((15,)),
            dma((len(LINKS), 2, PANELS)),
            dma((len(LINKS), 2, PANELS)),
            dma((PANELS,)),
            dma((PANELS,)),
        ],
        name="gather_panels",
        compiler_params=pltpu.CompilerParams(
            collective_id=0, has_side_effects=True, vmem_limit_bytes=36 * 2**20
        ),
    )(*(pltpu.with_memory_space_constraint(a, pltpu.HBM) for a in (counts, pairs, jnp.asarray(TABLE))))


def tile_kernel(tile_ref, panels_ref, out_ref, buffer, sem):
    first = pltpu.make_async_copy(tile_ref, out_ref.at[0, 0], sem.at[0])
    first.start()
    count = BLOCK // CHUNK

    def write(i):
        rows = pl.ds(i * CHUNK, CHUNK)
        return pltpu.make_async_copy(buffer.at[rows], out_ref.at[0, 1, rows], sem.at[1 + i])

    for i in range(count):
        rows = pl.ds(i * CHUNK, CHUNK)
        product = lax.dot_general(
            panels_ref[0, rows], panels_ref[1], (((1,), (1,)), ((), ())), preferred_element_type=jnp.float32
        )
        buffer[rows] = product.astype(jnp.bfloat16)
        write(i).start()
    first.wait()
    for i in range(count):
        write(i).wait()


def tiles(tile, panels):
    return pl.pallas_call(
        tile_kernel,
        out_shape=jax.ShapeDtypeStruct((1, 2, BLOCK, BLOCK), jnp.bfloat16),
        in_specs=[pl.BlockSpec(memory_space=pl.ANY), pl.BlockSpec(memory_space=pltpu.VMEM)],
        out_specs=pl.BlockSpec(memory_space=pl.ANY),
        scratch_shapes=[
            pltpu.VMEM((BLOCK, BLOCK), jnp.bfloat16),
            pltpu.SemaphoreType.DMA((1 + BLOCK // CHUNK,)),
        ],
        name="tile_products",
        compiler_params=pltpu.CompilerParams(vmem_limit_bytes=24 * 2**20),
    )(tile, panels)


def on_device(genotypes, pairs):
    by_panel = pairs.transpose(1, 2, 0).reshape(PANELS, -1)
    return tiles(*gather(genotypes, by_panel))


def solution(mesh):
    return jax.shard_map(
        on_device,
        mesh=mesh,
        in_specs=(P(("row", "col"), None), P()),
        out_specs=P(("row", "col"), None, None, None),
        check_vma=False,
    )
```

```python
import jax
import jax.numpy as jnp
import numpy as np
from jax import lax
from jax.experimental import pallas as pl
from jax.experimental.pallas import tpu as pltpu
from jax.sharding import PartitionSpec as P

MESH = pl.DeviceIdType.MESH
SNPS = 512
RING = 4
ROW_COUNT = 16
COL_COUNT = 8
SHARD = 256
SAMPLES = SHARD * ROW_COUNT * COL_COUNT
BLOCK = SHARD * COL_COUNT
STREAMS = 2
PARTS = 2
PIECE = SHARD // (STREAMS * PARTS)
PANELS = 4
LINKS = ((1, 0, 0), (3, 0, 0), (0, 1, 0), (0, 3, 0), (0, 0, 1), (0, 0, 3))
PER_LINK = 2
CHUNK = 512

RELAYS = (
    ((1, 16), (0, 48), (0, 4), (1, 12), (1, 1), (0, 3)),
    ((0, 20), (1, 60), (0, 52), (1, 28), (0, 49), (1, 19)),
    ((0, 36), (1, 44), (1, 5), (0, 15), (0, 21), (1, 63)),
    ((1, 35), (0, 33), (0, 24), (1, 56), (1, 29), (0, 55)),
    ((0, 40), (1, 40), (0, 25), (1, 59), (0, 34), (1, 34)),
    ((1, 11), (0, 9), (1, 38), (0, 46), (1, 30), (0, 54)),
)
DIRECT = (
    ((0, 1), (0, 6), (0, 19), (0, 31), (0, 37), (0, 41), (0, 56), (0, 62), (1, 8), (1, 15), (1, 21), (1, 27), (1, 32), (1, 45), (1, 50), (1, 54)),
    ((0, 5), (0, 8), (0, 18), (0, 30), (0, 32), (0, 39), (0, 57), (0, 63), (1, 3), (1, 14), (1, 22), (1, 24), (1, 43), (1, 47), (1, 49), (1, 53)),
    ((0, 13), (0, 28), (0, 29), (0, 38), (0, 44), (0, 58), (0, 59), (1, 4), (1, 9), (1, 20), (1, 23), (1, 42), (1, 48), (1, 51)),
    ((0, 11), (0, 12), (0, 16), (0, 17), (0, 42), (0, 60), (0, 61), (1, 7), (1, 25), (1, 26), (1, 36), (1, 46), (1, 52), (1, 55)),
    ((0, 10), (0, 22), (0, 26), (0, 35), (0, 47), (0, 50), (0, 53), (1, 2), (1, 6), (1, 13), (1, 17), (1, 39), (1, 41), (1, 57), (1, 61)),
    ((0, 2), (0, 7), (0, 14), (0, 23), (0, 27), (0, 43), (0, 45), (0, 51), (1, 10), (1, 18), (1, 31), (1, 33), (1, 37), (1, 58), (1, 62)),
)


def offset_of(n):
    return n // (RING * RING), n // RING % RING, n % RING


def number(offset):
    return (offset[0] * RING + offset[1]) * RING + offset[2]


def before(n, link):
    return number(tuple((i - j) % RING for i, j in zip(offset_of(n), LINKS[link])))


HELD = tuple((p, 0) for p in range(PARTS)) + tuple(item for step in RELAYS for item in step)
LANES = 128
SLOT_OF = {item: i for i, item in enumerate(HELD)}
CAME_BY = {item: link for step in RELAYS for link, item in enumerate(step)}


def class_of(n, y_lo):
    dx, dy, _ = offset_of(n)
    return (dx * 2 + y_lo) * 2 + ((dy + 1 - y_lo) // 2) % 2


def tables():
    table = np.zeros((18, LANES), np.int32)
    own_most = 0
    for y_lo in range(2):
        for kind in sorted({class_of(n, y_lo) for n in range(RING**3)}):
            places = []
            for e, items in enumerate(DIRECT):
                mine = [(p, n) for p, n in items if class_of(n, y_lo) == kind]
                assert len(mine) <= PER_LINK
                places += [(e * PER_LINK + i, SLOT_OF[p, before(n, e)], p, n) for i, (p, n) in enumerate(mine)]
            own = [(slot, p, n) for slot, (p, n) in enumerate(HELD) if class_of(n, y_lo) == kind]
            own_most = max(own_most, len(own))
            places += [(FROM_LINKS + i, *one) for i, one in enumerate(own)]
            assert len(places) == PARTS * COL_COUNT
            for place, slot, p, n in places:
                table[kind, place] = slot
                table[16 + y_lo, p * RING**3 + n] = place
    return table, own_most


FROM_LINKS = len(LINKS) * PER_LINK
TABLE, OWN = tables()
PIECES = FROM_LINKS + OWN


def place_of_self():
    row, col = lax.axis_index("row"), lax.axis_index("col")
    return (row // 2) % RING, (row // 8) * 2 + col // RING, col % RING, row % 2


def kind_of(block, x, y):
    behind = (x - lax.shift_right_logical(block, 1)) & (RING - 1)
    half = ((y // 2) - lax.shift_right_logical(block, 3)) & 1
    return (behind * 2 + y % 2) * 2 + half


def gather_kernel(
    counts_hbm, pairs_hbm, table_hbm, tile_ref, panels_ref,
    counts_ref, pairs_ref, table_ref, held, sums, away, near, landed0, landed1, landed2, landed3, left, right,
    load_sem, twin_send, twin_recv, relay_send, relay_recv, stat_send, stat_recv,
    link_send, link_recv, near_send, near_recv,
):
    x, y, z, core = place_of_self()
    landed = (landed0, landed1, landed2, landed3)

    def place(offset):
        return tuple((me + step) % RING for me, step in zip((x, y, z), offset))

    def device_at(offset, on_core):
        px, py, pz = place(offset)
        return ((py // 2) * RING + px) * 2 + on_core, (py % 2) * RING + pz

    here = (0, 0, 0)
    twin = device_at(here, 1 - core)
    neighbours = [device_at(link, core) for link in LINKS]
    across = [device_at(tuple(2 * (a == axis) for a in range(3)), core) for axis in range(3)]
    others = [device_at(link, 1 - core) for link in LINKS]

    barrier = pltpu.get_barrier_semaphore()
    peers = [twin, *neighbours, *others, *across]
    for peer in peers:
        pl.semaphore_signal(barrier, inc=1, device_id=peer, device_id_type=MESH)

    mine, theirs = core * (SHARD // 2), (1 - core) * (SHARD // 2)
    quarters = [pl.ds(pl.multiple_of(half + p * PIECE, PIECE), PIECE) for half in (theirs, mine) for p in range(PARTS)]
    loads = [
        pltpu.make_async_copy(source, target, load_sem.at[i])
        for i, (source, target) in enumerate(
            [(counts_hbm.at[rows], counts_ref.at[rows]) for rows in quarters]
            + [(pairs_hbm, pairs_ref), (table_hbm, table_ref)]
        )
    ]
    for load in loads:
        load.start()
    for i, rows in enumerate(quarters):
        loads[i].wait()
        quarter = counts_ref[rows].astype(jnp.float32).astype(jnp.bfloat16)
        if i < PARTS:
            near[2, i] = quarter
        else:
            held[i - PARTS, core] = quarter
    halves = (core, 1 - core)

    def swap(p, half):
        return pltpu.make_async_remote_copy(
            src_ref=near.at[2, p],
            dst_ref=held.at[p, half],
            send_sem=twin_send.at[p],
            recv_sem=twin_recv.at[p],
            device_id=twin,
            device_id_type=MESH,
        )

    pl.semaphore_wait(barrier, len(peers))
    for p in range(PARTS):
        swap(p, core).start()

    def sum_to(slot, source, target):
        return pltpu.make_async_remote_copy(
            src_ref=sums.at[source],
            dst_ref=sums.at[slot],
            send_sem=stat_send.at[slot],
            recv_sem=stat_recv.at[slot],
            device_id=target,
            device_id_type=MESH,
        )

    def stat_copies(phase):
        if phase == 0:
            return [sum_to(1, 0, twin)]
        axis, base = phase - 1, 4 * phase - 2
        targets = [neighbours[2 * axis], neighbours[2 * axis + 1], across[axis]]
        return [sum_to(base + 1 + i, base, target) for i, target in enumerate(targets)]

    def stat_finish(phase):
        for copy in stat_copies(phase):
            copy.wait()
        if phase == 0:
            sums[2] = sums[0] + sums[1]
        else:
            base = 4 * phase - 2
            sums[base + 4] = (sums[base] + sums[base + 1]) + (sums[base + 2] + sums[base + 3])

    def stat_start():
        counts = counts_ref[...]
        total = jnp.sum(counts, axis=0, keepdims=True)
        square = jnp.sum(counts * counts, axis=0, keepdims=True)
        which = lax.broadcasted_iota(jnp.int32, (8, SNPS), 0)
        sums[0] = jnp.where(which == 0, total, jnp.where(which == 1, square, 0))
        for copy in stat_copies(0):
            copy.start()

    def relay(item, half):
        slot, link = SLOT_OF[item], CAME_BY[item]
        source = SLOT_OF[item[0], before(item[1], link)]
        return pltpu.make_async_remote_copy(
            src_ref=held.at[source, halves[half]],
            dst_ref=held.at[slot, halves[half]],
            send_sem=relay_send.at[slot, half],
            recv_sem=relay_recv.at[slot, half],
            device_id=neighbours[link],
            device_id_type=MESH,
        )

    arrived = {((p, 0), 0) for p in range(PARTS)}

    def arrive(item, half):
        if (item, half) not in arrived:
            arrived.add((item, half))
            if item[1] == 0:
                swap(item[0], halves[1]).wait_recv()
            else:
                relay(item, half).wait_recv()

    for t, step in enumerate(RELAYS):
        for half in range(2):
            for link, item in enumerate(step):
                arrive((item[0], before(item[1], link)), half)
                relay(item, half).start()
            if t == 0 and half == 0:
                stat_start()
        if 0 < t < 5:
            stat_finish(t - 1)
            if t < 4:
                for copy in stat_copies(t):
                    copy.start()
    for step in RELAYS:
        for half in range(2):
            for item in step:
                arrive(item, half)
    loads[4].wait()
    loads[5].wait()

    total, square = sums[14, 0:1], sums[14, 1:2]
    shifted = total - SAMPLES
    spread = SAMPLES * (square - 2 * total + SAMPLES) - shifted * shifted
    variance = spread.astype(jnp.float32) * (1.0 / (float(SAMPLES) * SAMPLES)) + 1e-05
    mean = total.astype(jnp.float32) * (1.0 / SAMPLES)
    scale = lax.rsqrt(variance)

    def standard(slot, half, factor):
        return ((held[slot, half].astype(jnp.float32) - mean) * (scale * factor)).astype(jnp.bfloat16)

    def wanted(device, panel):
        return jnp.maximum(pairs_ref[panel, device[0] * COL_COUNT + device[1]], 0)

    def step_of(link):
        step = 1 + 2 * (link % 2)
        return tuple(jnp.where(link // 2 == axis, step, 0) for axis in range(3))

    def to_link(link, to_core, panel, stream):
        return pltpu.make_async_remote_copy(
            src_ref=away.at[link, to_core, panel % 2],
            dst_ref=landed[panel].at[stream, pl.ds(link * PER_LINK, PER_LINK)],
            send_sem=link_send.at[link, to_core, panel],
            recv_sem=link_recv.at[link, stream, panel],
            device_id=device_at(step_of(link), to_core),
            device_id_type=MESH,
        )

    def to_twin(panel, stream):
        return pltpu.make_async_remote_copy(
            src_ref=near.at[panel % 2],
            dst_ref=landed[panel].at[stream, pl.ds(FROM_LINKS, OWN)],
            send_sem=near_send.at[panel],
            recv_sem=near_recv.at[panel],
            device_id=twin,
            device_id_type=MESH,
        )

    def sent(panel):
        for link in range(len(LINKS)):
            for to_core in range(2):
                to_link(link, to_core, panel, core).wait_send()
        to_twin(panel, core).wait_send()

    def send_panel(panel):
        if panel >= 2:
            sent(panel - 2)
        factor = 1.0 / SNPS if panel % 2 == 0 else 1.0

        def message(m, carry):
            to_core, link = m // len(LINKS), m % len(LINKS)
            step = step_of(link)
            block = wanted(device_at(step, to_core), panel)
            px, py, _ = place(step)
            kind = kind_of(block, px, py)
            for i in range(PER_LINK):
                slot = table_ref[kind, link * PER_LINK + i]
                away[link, to_core, panel % 2, i] = standard(slot, block & 1, factor)
            to_link(link, to_core, panel, core).start()
            return carry

        lax.fori_loop(0, 2 * len(LINKS), message, 0)
        for device in (twin, device_at(here, core)):
            block = wanted(device, panel)
            kind = kind_of(block, x, y)

            def one(i, carry):
                piece = standard(table_ref[kind, FROM_LINKS + i], block & 1, factor)
                if device is twin:
                    near[panel % 2, i] = piece
                else:
                    landed[panel][core, FROM_LINKS + i] = piece
                return carry

            lax.fori_loop(0, OWN, one, 0)
            if device is twin:
                to_twin(panel, core).start()

    for panel in range(PANELS):
        send_panel(panel)

    def in_order(panel, target):
        for link in range(len(LINKS)):
            for stream in range(STREAMS):
                to_link(link, 0, panel, stream).wait_recv()
        to_twin(panel, 1 - core).wait_recv()
        block = wanted(device_at(here, core), panel)
        live = pairs_ref[panel, device_at(here, core)[0] * COL_COUNT + device_at(here, core)[1]] >= 0
        keep = jnp.where(live, 1.0, 0.0).astype(jnp.bfloat16)
        dx = (x - lax.shift_right_logical(block, 1)) & (RING - 1)

        def one(col, carry):
            dy = (y - (2 * lax.shift_right_logical(block, 3) + col // RING)) & (RING - 1)
            dz = (z - col % RING) & (RING - 1)
            for p in range(PARTS):
                place = table_ref[16 + y % 2, p * RING**3 + (dx * RING + dy) * RING + dz]
                for stream in range(STREAMS):
                    first = col * SHARD + stream * (SHARD // 2) + p * PIECE
                    rows = pl.ds(pl.multiple_of(first, PIECE), PIECE)
                    piece = landed[panel][stream, place]
                    target[rows] = piece * keep if panel % 2 == 0 else piece
            return carry

        lax.fori_loop(0, COL_COUNT, one, 0)

    for p in range(PARTS):
        swap(p, core).wait_send()
    for step in RELAYS:
        for half in range(2):
            for item in step:
                relay(item, half).wait_send()
    in_order(0, left)
    in_order(1, right)

    def multiply(i, carry):
        rows = pl.ds(pl.multiple_of(i * CHUNK, CHUNK), CHUNK)
        product = lax.dot_general(
            left[rows], right[...], (((1,), (1,)), ((), ())), preferred_element_type=jnp.float32
        )
        tile_ref[rows] = product.astype(jnp.bfloat16)
        return carry

    lax.fori_loop(0, BLOCK // CHUNK, multiply, 0)
    in_order(2, panels_ref.at[0])
    in_order(3, panels_ref.at[1])
    for panel in (2, 3):
        sent(panel)


def gather(counts, pairs):
    dma = pltpu.SemaphoreType.DMA
    bf16 = jnp.bfloat16
    return pl.pallas_call(
        gather_kernel,
        out_shape=(
            jax.ShapeDtypeStruct((BLOCK, BLOCK), bf16),
            jax.ShapeDtypeStruct((2, BLOCK, SNPS), bf16),
        ),
        in_specs=[pl.BlockSpec(memory_space=pltpu.HBM)] * 3,
        out_specs=(pl.BlockSpec(memory_space=pltpu.VMEM),) * 2,
        scratch_shapes=[
            pltpu.VMEM((SHARD, SNPS), jnp.int32),
            pltpu.SMEM((PANELS, LANES), jnp.int32),
            pltpu.SMEM(TABLE.shape, jnp.int32),
            pltpu.VMEM((len(HELD), 2, PIECE, SNPS), bf16),
            pltpu.VMEM((15, 8, SNPS), jnp.int32),
            pltpu.VMEM((len(LINKS), 2, 2, PER_LINK, PIECE, SNPS), bf16),
            pltpu.VMEM((3, OWN, PIECE, SNPS), bf16),
            *[pltpu.VMEM((STREAMS, PIECES, PIECE, SNPS), bf16) for _ in range(PANELS)],
            pltpu.VMEM((BLOCK, SNPS), bf16),
            pltpu.VMEM((BLOCK, SNPS), bf16),
            dma((6,)),
            dma((PARTS,)),
            dma((PARTS,)),
            dma((len(HELD), 2)),
            dma((len(HELD), 2)),
            dma((15,)),
            dma((15,)),
            dma((len(LINKS), 2, PANELS)),
            dma((len(LINKS), 2, PANELS)),
            dma((PANELS,)),
            dma((PANELS,)),
        ],
        name="gather_panels",
        compiler_params=pltpu.CompilerParams(
            collective_id=0, has_side_effects=True, vmem_limit_bytes=36 * 2**20
        ),
    )(*(pltpu.with_memory_space_constraint(a, pltpu.HBM) for a in (counts, pairs, jnp.asarray(TABLE))))


def tile_kernel(tile_ref, panels_ref, out_ref, buffer, sem):
    first = pltpu.make_async_copy(tile_ref, out_ref.at[0, 0], sem.at[0])
    first.start()
    count = BLOCK // CHUNK

    def write(i):
        rows = pl.ds(i * CHUNK, CHUNK)
        return pltpu.make_async_copy(buffer.at[rows], out_ref.at[0, 1, rows], sem.at[1 + i])

    for i in range(count):
        rows = pl.ds(i * CHUNK, CHUNK)
        product = lax.dot_general(
            panels_ref[0, rows], panels_ref[1], (((1,), (1,)), ((), ())), preferred_element_type=jnp.float32
        )
        buffer[rows] = product.astype(jnp.bfloat16)
        write(i).start()
    first.wait()
    for i in range(count):
        write(i).wait()


def tiles(tile, panels):
    return pl.pallas_call(
        tile_kernel,
        out_shape=jax.ShapeDtypeStruct((1, 2, BLOCK, BLOCK), jnp.bfloat16),
        in_specs=[pl.BlockSpec(memory_space=pl.ANY), pl.BlockSpec(memory_space=pltpu.VMEM)],
        out_specs=pl.BlockSpec(memory_space=pl.ANY),
        scratch_shapes=[
            pltpu.VMEM((BLOCK, BLOCK), jnp.bfloat16),
            pltpu.SemaphoreType.DMA((1 + BLOCK // CHUNK,)),
        ],
        name="tile_products",
        compiler_params=pltpu.CompilerParams(vmem_limit_bytes=24 * 2**20),
    )(tile, panels)


def on_device(genotypes, pairs):
    by_panel = pairs.transpose(1, 2, 0).reshape(PANELS, -1)
    return tiles(*gather(genotypes, by_panel))


def solution(mesh):
    return jax.shard_map(
        on_device,
        mesh=mesh,
        in_specs=(P(("row", "col"), None), P()),
        out_specs=P(("row", "col"), None, None, None),
        check_vma=False,
    )
```

```python
import jax
import jax.numpy as jnp
import numpy as np
from jax import lax
from jax.experimental import pallas as pl
from jax.experimental.pallas import tpu as pltpu
from jax.sharding import PartitionSpec as P

MESH = pl.DeviceIdType.MESH
SNPS = 512
RING = 4
ROW_COUNT = 16
COL_COUNT = 8
SHARD = 256
SAMPLES = SHARD * ROW_COUNT * COL_COUNT
BLOCK = SHARD * COL_COUNT
STREAMS = 2
PARTS = 2
PIECE = SHARD // (STREAMS * PARTS)
PANELS = 4
LINKS = ((1, 0, 0), (3, 0, 0), (0, 1, 0), (0, 3, 0), (0, 0, 1), (0, 0, 3))
PER_LINK = 2
CHUNK = 512

RELAYS = (
    ((1, 16), (0, 48), (0, 4), (1, 12), (1, 1), (0, 3)),
    ((0, 20), (1, 60), (0, 52), (1, 28), (0, 49), (1, 19)),
    ((0, 36), (1, 44), (1, 5), (0, 15), (0, 21), (1, 63)),
    ((1, 35), (0, 33), (0, 24), (1, 56), (1, 29), (0, 55)),
    ((0, 40), (1, 40), (0, 25), (1, 59), (0, 34), (1, 34)),
    ((1, 11), (0, 9), (1, 38), (0, 46), (1, 30), (0, 54)),
)
DIRECT = (
    ((0, 1), (0, 6), (0, 19), (0, 31), (0, 37), (0, 41), (0, 56), (0, 62), (1, 8), (1, 15), (1, 21), (1, 27), (1, 32), (1, 45), (1, 50), (1, 54)),
    ((0, 5), (0, 8), (0, 18), (0, 30), (0, 32), (0, 39), (0, 57), (0, 63), (1, 3), (1, 14), (1, 22), (1, 24), (1, 43), (1, 47), (1, 49), (1, 53)),
    ((0, 13), (0, 28), (0, 29), (0, 38), (0, 44), (0, 58), (0, 59), (1, 4), (1, 9), (1, 20), (1, 23), (1, 42), (1, 48), (1, 51)),
    ((0, 11), (0, 12), (0, 16), (0, 17), (0, 42), (0, 60), (0, 61), (1, 7), (1, 25), (1, 26), (1, 36), (1, 46), (1, 52), (1, 55)),
    ((0, 10), (0, 22), (0, 26), (0, 35), (0, 47), (0, 50), (0, 53), (1, 2), (1, 6), (1, 13), (1, 17), (1, 39), (1, 41), (1, 57), (1, 61)),
    ((0, 2), (0, 7), (0, 14), (0, 23), (0, 27), (0, 43), (0, 45), (0, 51), (1, 10), (1, 18), (1, 31), (1, 33), (1, 37), (1, 58), (1, 62)),
)

ORDER = (
    0, 2, 4, 6, 8, 10, 1, 3, 5, 7, 9, 11, 18, 22, 16, 20, 12, 14,
    19, 23, 17, 21, 13, 15, 30, 29, 44, 36, 46, 38, 42, 40, 32, 37, 34, 39,
    43, 41, 33, 25, 35, 27, 31, 28, 45, 24, 58, 50, 52, 54, 57, 48, 59, 51,
    53, 55, 56, 49, 47, 26, 64, 69, 70, 62, 60, 67, 65, 68, 63, 61, 66, 71,
)


def offset_of(n):
    return n // (RING * RING), n // RING % RING, n % RING


def number(offset):
    return (offset[0] * RING + offset[1]) * RING + offset[2]


def before(n, link):
    return number(tuple((i - j) % RING for i, j in zip(offset_of(n), LINKS[link])))


HELD = tuple((p, 0) for p in range(PARTS)) + tuple(item for step in RELAYS for item in step)
LANES = 128
SLOT_OF = {item: i for i, item in enumerate(HELD)}
CAME_BY = {item: link for step in RELAYS for link, item in enumerate(step)}


def class_of(n, y_lo):
    dx, dy, _ = offset_of(n)
    return (dx * 2 + y_lo) * 2 + ((dy + 1 - y_lo) // 2) % 2


def tables():
    table = np.zeros((18, LANES), np.int32)
    own_most = 0
    for y_lo in range(2):
        for kind in sorted({class_of(n, y_lo) for n in range(RING**3)}):
            places = []
            for e, items in enumerate(DIRECT):
                mine = [(p, n) for p, n in items if class_of(n, y_lo) == kind]
                assert len(mine) <= PER_LINK
                places += [(e * PER_LINK + i, SLOT_OF[p, before(n, e)], p, n) for i, (p, n) in enumerate(mine)]
            own = [(slot, p, n) for slot, (p, n) in enumerate(HELD) if class_of(n, y_lo) == kind]
            own_most = max(own_most, len(own))
            places += [(FROM_LINKS + i, *one) for i, one in enumerate(own)]
            assert len(places) == PARTS * COL_COUNT
            for place, slot, p, n in places:
                table[kind, place] = slot
                table[16 + y_lo, p * RING**3 + n] = place
    return table, own_most


FROM_LINKS = len(LINKS) * PER_LINK
TABLE, OWN = tables()
PIECES = FROM_LINKS + OWN


def place_of_self():
    row, col = lax.axis_index("row"), lax.axis_index("col")
    return (row // 2) % RING, (row // 8) * 2 + col // RING, col % RING, row % 2


def kind_of(block, x, y):
    behind = (x - lax.shift_right_logical(block, 1)) & (RING - 1)
    half = ((y // 2) - lax.shift_right_logical(block, 3)) & 1
    return (behind * 2 + y % 2) * 2 + half


def gather_kernel(
    counts_hbm, pairs_hbm, table_hbm, tile_ref, panels_ref,
    counts_ref, pairs_ref, table_ref, held, sums, away, near, landed0, landed1, landed2, landed3, left, right,
    load_sem, twin_send, twin_recv, relay_send, relay_recv, stat_send, stat_recv,
    link_send, link_recv, near_send, near_recv,
):
    x, y, z, core = place_of_self()
    landed = (landed0, landed1, landed2, landed3)

    def place(offset):
        return tuple((me + step) % RING for me, step in zip((x, y, z), offset))

    def device_at(offset, on_core):
        px, py, pz = place(offset)
        return ((py // 2) * RING + px) * 2 + on_core, (py % 2) * RING + pz

    here = (0, 0, 0)
    twin = device_at(here, 1 - core)
    neighbours = [device_at(link, core) for link in LINKS]
    across = [device_at(tuple(2 * (a == axis) for a in range(3)), core) for axis in range(3)]
    others = [device_at(link, 1 - core) for link in LINKS]

    barrier = pltpu.get_barrier_semaphore()
    peers = [twin, *neighbours, *others, *across]
    for peer in peers:
        pl.semaphore_signal(barrier, inc=1, device_id=peer, device_id_type=MESH)

    mine, theirs = core * (SHARD // 2), (1 - core) * (SHARD // 2)
    quarters = [pl.ds(pl.multiple_of(half + p * PIECE, PIECE), PIECE) for half in (theirs, mine) for p in range(PARTS)]
    loads = [
        pltpu.make_async_copy(source, target, load_sem.at[i])
        for i, (source, target) in enumerate(
            [(counts_hbm.at[rows], counts_ref.at[rows]) for rows in quarters]
            + [(pairs_hbm, pairs_ref), (table_hbm, table_ref)]
        )
    ]
    for load in loads:
        load.start()
    for i, rows in enumerate(quarters):
        loads[i].wait()
        quarter = counts_ref[rows].astype(jnp.float32).astype(jnp.bfloat16)
        if i < PARTS:
            near[2, i] = quarter
        else:
            held[i - PARTS, core] = quarter
    halves = (core, 1 - core)

    def swap(p, half):
        return pltpu.make_async_remote_copy(
            src_ref=near.at[2, p],
            dst_ref=held.at[p, half],
            send_sem=twin_send.at[p],
            recv_sem=twin_recv.at[p],
            device_id=twin,
            device_id_type=MESH,
        )

    pl.semaphore_wait(barrier, len(peers))
    for p in range(PARTS):
        swap(p, core).start()

    def sum_to(slot, source, target):
        return pltpu.make_async_remote_copy(
            src_ref=sums.at[source],
            dst_ref=sums.at[slot],
            send_sem=stat_send.at[slot],
            recv_sem=stat_recv.at[slot],
            device_id=target,
            device_id_type=MESH,
        )

    def stat_copies(phase):
        if phase == 0:
            return [sum_to(1, 0, twin)]
        axis, base = phase - 1, 4 * phase - 2
        targets = [neighbours[2 * axis], neighbours[2 * axis + 1], across[axis]]
        return [sum_to(base + 1 + i, base, target) for i, target in enumerate(targets)]

    def stat_finish(phase):
        for copy in stat_copies(phase):
            copy.wait()
        if phase == 0:
            sums[2] = sums[0] + sums[1]
        else:
            base = 4 * phase - 2
            sums[base + 4] = (sums[base] + sums[base + 1]) + (sums[base + 2] + sums[base + 3])

    def stat_start():
        counts = counts_ref[...]
        total = jnp.sum(counts, axis=0, keepdims=True)
        square = jnp.sum(counts * counts, axis=0, keepdims=True)
        which = lax.broadcasted_iota(jnp.int32, (8, SNPS), 0)
        sums[0] = jnp.where(which == 0, total, jnp.where(which == 1, square, 0))
        for copy in stat_copies(0):
            copy.start()

    def relay(item, half):
        slot, link = SLOT_OF[item], CAME_BY[item]
        source = SLOT_OF[item[0], before(item[1], link)]
        return pltpu.make_async_remote_copy(
            src_ref=held.at[source, halves[half]],
            dst_ref=held.at[slot, halves[half]],
            send_sem=relay_send.at[slot, half],
            recv_sem=relay_recv.at[slot, half],
            device_id=neighbours[link],
            device_id_type=MESH,
        )

    arrived = {((p, 0), 0) for p in range(PARTS)}

    def arrive(item, half):
        if (item, half) not in arrived:
            arrived.add((item, half))
            if item[1] == 0:
                swap(item[0], halves[1]).wait_recv()
            else:
                relay(item, half).wait_recv()

    for i, code in enumerate(ORDER):
        item, half = HELD[PARTS + code // 2], code % 2
        arrive((item[0], before(item[1], CAME_BY[item])), half)
        relay(item, half).start()
        if i == len(LINKS) - 1:
            stat_start()
        t, last = divmod(i, 2 * len(LINKS))
        if last == 2 * len(LINKS) - 1 and 0 < t < 5:
            stat_finish(t - 1)
            if t < 4:
                for copy in stat_copies(t):
                    copy.start()
    for step in RELAYS:
        for half in range(2):
            for item in step:
                arrive(item, half)
    loads[4].wait()
    loads[5].wait()

    total, square = sums[14, 0:1], sums[14, 1:2]
    shifted = total - SAMPLES
    spread = SAMPLES * (square - 2 * total + SAMPLES) - shifted * shifted
    variance = spread.astype(jnp.float32) * (1.0 / (float(SAMPLES) * SAMPLES)) + 1e-05
    mean = total.astype(jnp.float32) * (1.0 / SAMPLES)
    scale = lax.rsqrt(variance)

    def standard(slot, half, factor):
        return ((held[slot, half].astype(jnp.float32) - mean) * (scale * factor)).astype(jnp.bfloat16)

    def wanted(device, panel):
        return jnp.maximum(pairs_ref[panel, device[0] * COL_COUNT + device[1]], 0)

    def step_of(link):
        step = 1 + 2 * (link % 2)
        return tuple(jnp.where(link // 2 == axis, step, 0) for axis in range(3))

    def to_link(link, to_core, panel, stream):
        return pltpu.make_async_remote_copy(
            src_ref=away.at[link, to_core, panel % 2],
            dst_ref=landed[panel].at[stream, pl.ds(link * PER_LINK, PER_LINK)],
            send_sem=link_send.at[link, to_core, panel],
            recv_sem=link_recv.at[link, stream, panel],
            device_id=device_at(step_of(link), to_core),
            device_id_type=MESH,
        )

    def to_twin(panel, stream):
        return pltpu.make_async_remote_copy(
            src_ref=near.at[panel % 2],
            dst_ref=landed[panel].at[stream, pl.ds(FROM_LINKS, OWN)],
            send_sem=near_send.at[panel],
            recv_sem=near_recv.at[panel],
            device_id=twin,
            device_id_type=MESH,
        )

    def sent(panel):
        for link in range(len(LINKS)):
            for to_core in range(2):
                to_link(link, to_core, panel, core).wait_send()
        to_twin(panel, core).wait_send()

    def send_panel(panel):
        if panel >= 2:
            sent(panel - 2)
        factor = 1.0 / SNPS if panel % 2 == 0 else 1.0

        def message(m, carry):
            to_core, link = m // len(LINKS), m % len(LINKS)
            step = step_of(link)
            block = wanted(device_at(step, to_core), panel)
            px, py, _ = place(step)
            kind = kind_of(block, px, py)
            for i in range(PER_LINK):
                slot = table_ref[kind, link * PER_LINK + i]
                away[link, to_core, panel % 2, i] = standard(slot, block & 1, factor)
            to_link(link, to_core, panel, core).start()
            return carry

        lax.fori_loop(0, 2 * len(LINKS), message, 0)
        for device in (twin, device_at(here, core)):
            block = wanted(device, panel)
            kind = kind_of(block, x, y)

            def one(i, carry):
                piece = standard(table_ref[kind, FROM_LINKS + i], block & 1, factor)
                if device is twin:
                    near[panel % 2, i] = piece
                else:
                    landed[panel][core, FROM_LINKS + i] = piece
                return carry

            lax.fori_loop(0, OWN, one, 0)
            if device is twin:
                to_twin(panel, core).start()

    for panel in range(PANELS):
        send_panel(panel)

    def in_order(panel, target):
        for link in range(len(LINKS)):
            for stream in range(STREAMS):
                to_link(link, 0, panel, stream).wait_recv()
        to_twin(panel, 1 - core).wait_recv()
        block = wanted(device_at(here, core), panel)
        live = pairs_ref[panel, device_at(here, core)[0] * COL_COUNT + device_at(here, core)[1]] >= 0
        keep = jnp.where(live, 1.0, 0.0).astype(jnp.bfloat16)
        dx = (x - lax.shift_right_logical(block, 1)) & (RING - 1)

        def one(col, carry):
            dy = (y - (2 * lax.shift_right_logical(block, 3) + col // RING)) & (RING - 1)
            dz = (z - col % RING) & (RING - 1)
            for p in range(PARTS):
                place = table_ref[16 + y % 2, p * RING**3 + (dx * RING + dy) * RING + dz]
                for stream in range(STREAMS):
                    first = col * SHARD + stream * (SHARD // 2) + p * PIECE
                    rows = pl.ds(pl.multiple_of(first, PIECE), PIECE)
                    piece = landed[panel][stream, place]
                    target[rows] = piece * keep if panel % 2 == 0 else piece
            return carry

        lax.fori_loop(0, COL_COUNT, one, 0)

    for p in range(PARTS):
        swap(p, core).wait_send()
    for step in RELAYS:
        for half in range(2):
            for item in step:
                relay(item, half).wait_send()
    in_order(0, left)
    in_order(1, right)

    def multiply(i, carry):
        rows = pl.ds(pl.multiple_of(i * CHUNK, CHUNK), CHUNK)
        product = lax.dot_general(
            left[rows], right[...], (((1,), (1,)), ((), ())), preferred_element_type=jnp.float32
        )
        tile_ref[rows] = product.astype(jnp.bfloat16)
        return carry

    lax.fori_loop(0, BLOCK // CHUNK, multiply, 0)
    in_order(2, panels_ref.at[0])
    in_order(3, panels_ref.at[1])
    for panel in (2, 3):
        sent(panel)


def gather(counts, pairs):
    dma = pltpu.SemaphoreType.DMA
    bf16 = jnp.bfloat16
    return pl.pallas_call(
        gather_kernel,
        out_shape=(
            jax.ShapeDtypeStruct((BLOCK, BLOCK), bf16),
            jax.ShapeDtypeStruct((2, BLOCK, SNPS), bf16),
        ),
        in_specs=[pl.BlockSpec(memory_space=pltpu.HBM)] * 3,
        out_specs=(pl.BlockSpec(memory_space=pltpu.VMEM),) * 2,
        scratch_shapes=[
            pltpu.VMEM((SHARD, SNPS), jnp.int32),
            pltpu.SMEM((PANELS, LANES), jnp.int32),
            pltpu.SMEM(TABLE.shape, jnp.int32),
            pltpu.VMEM((len(HELD), 2, PIECE, SNPS), bf16),
            pltpu.VMEM((15, 8, SNPS), jnp.int32),
            pltpu.VMEM((len(LINKS), 2, 2, PER_LINK, PIECE, SNPS), bf16),
            pltpu.VMEM((3, OWN, PIECE, SNPS), bf16),
            *[pltpu.VMEM((STREAMS, PIECES, PIECE, SNPS), bf16) for _ in range(PANELS)],
            pltpu.VMEM((BLOCK, SNPS), bf16),
            pltpu.VMEM((BLOCK, SNPS), bf16),
            dma((6,)),
            dma((PARTS,)),
            dma((PARTS,)),
            dma((len(HELD), 2)),
            dma((len(HELD), 2)),
            dma((15,)),
            dma((15,)),
            dma((len(LINKS), 2, PANELS)),
            dma((len(LINKS), 2, PANELS)),
            dma((PANELS,)),
            dma((PANELS,)),
        ],
        name="gather_panels",
        compiler_params=pltpu.CompilerParams(
            collective_id=0, has_side_effects=True, vmem_limit_bytes=36 * 2**20
        ),
    )(*(pltpu.with_memory_space_constraint(a, pltpu.HBM) for a in (counts, pairs, jnp.asarray(TABLE))))


def tile_kernel(tile_ref, panels_ref, out_ref, buffer, sem):
    first = pltpu.make_async_copy(tile_ref, out_ref.at[0, 0], sem.at[0])
    first.start()
    count = BLOCK // CHUNK

    def write(i):
        rows = pl.ds(i * CHUNK, CHUNK)
        return pltpu.make_async_copy(buffer.at[rows], out_ref.at[0, 1, rows], sem.at[1 + i])

    for i in range(count):
        rows = pl.ds(i * CHUNK, CHUNK)
        product = lax.dot_general(
            panels_ref[0, rows], panels_ref[1], (((1,), (1,)), ((), ())), preferred_element_type=jnp.float32
        )
        buffer[rows] = product.astype(jnp.bfloat16)
        write(i).start()
    first.wait()
    for i in range(count):
        write(i).wait()


def tiles(tile, panels):
    return pl.pallas_call(
        tile_kernel,
        out_shape=jax.ShapeDtypeStruct((1, 2, BLOCK, BLOCK), jnp.bfloat16),
        in_specs=[pl.BlockSpec(memory_space=pl.ANY), pl.BlockSpec(memory_space=pltpu.VMEM)],
        out_specs=pl.BlockSpec(memory_space=pl.ANY),
        scratch_shapes=[
            pltpu.VMEM((BLOCK, BLOCK), jnp.bfloat16),
            pltpu.SemaphoreType.DMA((1 + BLOCK // CHUNK,)),
        ],
        name="tile_products",
        compiler_params=pltpu.CompilerParams(vmem_limit_bytes=24 * 2**20),
    )(tile, panels)


def on_device(genotypes, pairs):
    by_panel = pairs.transpose(1, 2, 0).reshape(PANELS, -1)
    return tiles(*gather(genotypes, by_panel))


def solution(mesh):
    return jax.shard_map(
        on_device,
        mesh=mesh,
        in_specs=(P(("row", "col"), None), P()),
        out_specs=P(("row", "col"), None, None, None),
        check_vma=False,
    )
```

```python
import jax
import jax.numpy as jnp
import numpy as np
from jax import lax
from jax.experimental import pallas as pl
from jax.experimental.pallas import tpu as pltpu
from jax.sharding import PartitionSpec as P

MESH = pl.DeviceIdType.MESH
SNPS = 512
RING = 4
ROW_COUNT = 16
COL_COUNT = 8
SHARD = 256
SAMPLES = SHARD * ROW_COUNT * COL_COUNT
BLOCK = SHARD * COL_COUNT
STREAMS = 2
PARTS = 2
PIECE = SHARD // (STREAMS * PARTS)
PANELS = 4
LINKS = ((1, 0, 0), (3, 0, 0), (0, 1, 0), (0, 3, 0), (0, 0, 1), (0, 0, 3))
PER_LINK = 2
CHUNK = 512
STAT_AFTER = (20, 38, 54, 71)

RELAYS = (
    ((1, 16), (0, 48), (0, 4), (1, 12), (1, 1), (0, 3)),
    ((0, 20), (1, 60), (0, 52), (1, 28), (0, 49), (1, 19)),
    ((0, 36), (1, 44), (1, 5), (0, 15), (0, 21), (1, 63)),
    ((1, 35), (0, 33), (0, 24), (1, 56), (1, 29), (0, 55)),
    ((0, 40), (1, 40), (0, 25), (1, 59), (0, 34), (1, 34)),
    ((1, 11), (0, 9), (1, 38), (0, 46), (1, 30), (0, 54)),
)
DIRECT = (
    ((0, 1), (0, 6), (0, 19), (0, 31), (0, 37), (0, 41), (0, 56), (0, 62), (1, 8), (1, 15), (1, 21), (1, 27), (1, 32), (1, 45), (1, 50), (1, 54)),
    ((0, 5), (0, 8), (0, 18), (0, 30), (0, 32), (0, 39), (0, 57), (0, 63), (1, 3), (1, 14), (1, 22), (1, 24), (1, 43), (1, 47), (1, 49), (1, 53)),
    ((0, 13), (0, 28), (0, 29), (0, 38), (0, 44), (0, 58), (0, 59), (1, 4), (1, 9), (1, 20), (1, 23), (1, 42), (1, 48), (1, 51)),
    ((0, 11), (0, 12), (0, 16), (0, 17), (0, 42), (0, 60), (0, 61), (1, 7), (1, 25), (1, 26), (1, 36), (1, 46), (1, 52), (1, 55)),
    ((0, 10), (0, 22), (0, 26), (0, 35), (0, 47), (0, 50), (0, 53), (1, 2), (1, 6), (1, 13), (1, 17), (1, 39), (1, 41), (1, 57), (1, 61)),
    ((0, 2), (0, 7), (0, 14), (0, 23), (0, 27), (0, 43), (0, 45), (0, 51), (1, 10), (1, 18), (1, 31), (1, 33), (1, 37), (1, 58), (1, 62)),
)

ORDER = (
    0, 2, 4, 6, 8, 10, 1, 3, 5, 7, 9, 11, 18, 22, 16, 20, 12, 14,
    19, 23, 17, 21, 13, 15, 30, 29, 44, 36, 46, 38, 42, 40, 32, 37, 34, 39,
    43, 41, 33, 25, 35, 27, 31, 28, 45, 24, 58, 50, 52, 54, 57, 48, 59, 51,
    53, 55, 56, 49, 47, 26, 64, 69, 70, 62, 60, 67, 65, 68, 63, 61, 66, 71,
)


def offset_of(n):
    return n // (RING * RING), n // RING % RING, n % RING


def number(offset):
    return (offset[0] * RING + offset[1]) * RING + offset[2]


def before(n, link):
    return number(tuple((i - j) % RING for i, j in zip(offset_of(n), LINKS[link])))


HELD = tuple((p, 0) for p in range(PARTS)) + tuple(item for step in RELAYS for item in step)
LANES = 128
SLOT_OF = {item: i for i, item in enumerate(HELD)}
CAME_BY = {item: link for step in RELAYS for link, item in enumerate(step)}


def class_of(n, y_lo):
    dx, dy, _ = offset_of(n)
    return (dx * 2 + y_lo) * 2 + ((dy + 1 - y_lo) // 2) % 2


def tables():
    table = np.zeros((18, LANES), np.int32)
    own_most = 0
    for y_lo in range(2):
        for kind in sorted({class_of(n, y_lo) for n in range(RING**3)}):
            places = []
            for e, items in enumerate(DIRECT):
                mine = [(p, n) for p, n in items if class_of(n, y_lo) == kind]
                assert len(mine) <= PER_LINK
                places += [(e * PER_LINK + i, SLOT_OF[p, before(n, e)], p, n) for i, (p, n) in enumerate(mine)]
            own = [(slot, p, n) for slot, (p, n) in enumerate(HELD) if class_of(n, y_lo) == kind]
            own_most = max(own_most, len(own))
            places += [(FROM_LINKS + i, *one) for i, one in enumerate(own)]
            assert len(places) == PARTS * COL_COUNT
            for place, slot, p, n in places:
                table[kind, place] = slot
                table[16 + y_lo, p * RING**3 + n] = place
    return table, own_most


FROM_LINKS = len(LINKS) * PER_LINK
TABLE, OWN = tables()
PIECES = FROM_LINKS + OWN


def place_of_self():
    row, col = lax.axis_index("row"), lax.axis_index("col")
    return (row // 2) % RING, (row // 8) * 2 + col // RING, col % RING, row % 2


def kind_of(block, x, y):
    behind = (x - lax.shift_right_logical(block, 1)) & (RING - 1)
    half = ((y // 2) - lax.shift_right_logical(block, 3)) & 1
    return (behind * 2 + y % 2) * 2 + half


def gather_kernel(
    counts_hbm, pairs_hbm, table_hbm, tile_ref, panels_ref,
    counts_ref, pairs_ref, table_ref, held, sums, away, near, landed0, landed1, landed2, landed3, left, right,
    load_sem, twin_send, twin_recv, relay_send, relay_recv, stat_send, stat_recv,
    link_send, link_recv, near_send, near_recv,
):
    x, y, z, core = place_of_self()
    landed = (landed0, landed1, landed2, landed3)

    def place(offset):
        return tuple((me + step) % RING for me, step in zip((x, y, z), offset))

    def device_at(offset, on_core):
        px, py, pz = place(offset)
        return ((py // 2) * RING + px) * 2 + on_core, (py % 2) * RING + pz

    here = (0, 0, 0)
    twin = device_at(here, 1 - core)
    neighbours = [device_at(link, core) for link in LINKS]
    across = [device_at(tuple(2 * (a == axis) for a in range(3)), core) for axis in range(3)]
    others = [device_at(link, 1 - core) for link in LINKS]

    barrier = pltpu.get_barrier_semaphore()
    peers = [twin, *neighbours, *others, *across]

    mine, theirs = core * (SHARD // 2), (1 - core) * (SHARD // 2)
    quarters = [pl.ds(pl.multiple_of(half + p * PIECE, PIECE), PIECE) for half in (theirs, mine) for p in range(PARTS)]
    loads = [
        pltpu.make_async_copy(source, target, load_sem.at[i])
        for i, (source, target) in enumerate(
            [(counts_hbm.at[rows], counts_ref.at[rows]) for rows in quarters]
            + [(pairs_hbm, pairs_ref), (table_hbm, table_ref)]
        )
    ]
    for load in loads:
        load.start()
    for peer in peers:
        pl.semaphore_signal(barrier, inc=1, device_id=peer, device_id_type=MESH)
    for i, rows in enumerate(quarters):
        loads[i].wait()
        quarter = counts_ref[rows].astype(jnp.float32).astype(jnp.bfloat16)
        if i < PARTS:
            near[2, i] = quarter
        else:
            held[i - PARTS, core] = quarter
    halves = (core, 1 - core)

    def swap(p, half):
        return pltpu.make_async_remote_copy(
            src_ref=near.at[2, p],
            dst_ref=held.at[p, half],
            send_sem=twin_send.at[p],
            recv_sem=twin_recv.at[p],
            device_id=twin,
            device_id_type=MESH,
        )

    pl.semaphore_wait(barrier, len(peers))
    for p in range(PARTS):
        swap(p, core).start()

    def sum_to(slot, source, target):
        return pltpu.make_async_remote_copy(
            src_ref=sums.at[source],
            dst_ref=sums.at[slot],
            send_sem=stat_send.at[slot],
            recv_sem=stat_recv.at[slot],
            device_id=target,
            device_id_type=MESH,
        )

    def stat_copies(phase):
        if phase == 0:
            return [sum_to(1, 0, twin)]
        axis, base = phase - 1, 4 * phase - 2
        targets = [neighbours[2 * axis], neighbours[2 * axis + 1], across[axis]]
        return [sum_to(base + 1 + i, base, target) for i, target in enumerate(targets)]

    def stat_finish(phase):
        for copy in stat_copies(phase):
            copy.wait()
        if phase == 0:
            sums[2] = sums[0] + sums[1]
        else:
            base = 4 * phase - 2
            sums[base + 4] = (sums[base] + sums[base + 1]) + (sums[base + 2] + sums[base + 3])

    def stat_start():
        counts = counts_ref[...]
        total = jnp.sum(counts, axis=0, keepdims=True)
        square = jnp.sum(counts * counts, axis=0, keepdims=True)
        which = lax.broadcasted_iota(jnp.int32, (8, SNPS), 0)
        sums[0] = jnp.where(which == 0, total, jnp.where(which == 1, square, 0))
        for copy in stat_copies(0):
            copy.start()

    def relay(item, half):
        slot, link = SLOT_OF[item], CAME_BY[item]
        source = SLOT_OF[item[0], before(item[1], link)]
        return pltpu.make_async_remote_copy(
            src_ref=held.at[source, halves[half]],
            dst_ref=held.at[slot, halves[half]],
            send_sem=relay_send.at[slot, half],
            recv_sem=relay_recv.at[slot, half],
            device_id=neighbours[link],
            device_id_type=MESH,
        )

    arrived = {((p, 0), 0) for p in range(PARTS)}

    def arrive(item, half):
        if (item, half) not in arrived:
            arrived.add((item, half))
            if item[1] == 0:
                swap(item[0], halves[1]).wait_recv()
            else:
                relay(item, half).wait_recv()

    for i, code in enumerate(ORDER):
        item, half = HELD[PARTS + code // 2], code % 2
        arrive((item[0], before(item[1], CAME_BY[item])), half)
        relay(item, half).start()
        if i == len(LINKS) - 1:
            stat_start()
        if i in STAT_AFTER:
            t = STAT_AFTER.index(i) + 1
            stat_finish(t - 1)
            if t < 4:
                for copy in stat_copies(t):
                    copy.start()
    for step in RELAYS:
        for half in range(2):
            for item in step:
                arrive(item, half)
    loads[4].wait()
    loads[5].wait()

    total, square = sums[14, 0:1], sums[14, 1:2]
    shifted = total - SAMPLES
    spread = SAMPLES * (square - 2 * total + SAMPLES) - shifted * shifted
    variance = spread.astype(jnp.float32) * (1.0 / (float(SAMPLES) * SAMPLES)) + 1e-05
    mean = total.astype(jnp.float32) * (1.0 / SAMPLES)
    scale = lax.rsqrt(variance)

    def standard(slot, half, factor):
        return ((held[slot, half].astype(jnp.float32) - mean) * (scale * factor)).astype(jnp.bfloat16)

    def wanted(device, panel):
        return jnp.maximum(pairs_ref[panel, device[0] * COL_COUNT + device[1]], 0)

    def step_of(link):
        step = 1 + 2 * (link % 2)
        return tuple(jnp.where(link // 2 == axis, step, 0) for axis in range(3))

    def to_link(link, to_core, panel, stream):
        return pltpu.make_async_remote_copy(
            src_ref=away.at[link, to_core, panel % 2],
            dst_ref=landed[panel].at[stream, pl.ds(link * PER_LINK, PER_LINK)],
            send_sem=link_send.at[link, to_core, panel],
            recv_sem=link_recv.at[link, stream, panel],
            device_id=device_at(step_of(link), to_core),
            device_id_type=MESH,
        )

    def to_twin(panel, stream):
        return pltpu.make_async_remote_copy(
            src_ref=near.at[panel % 2],
            dst_ref=landed[panel].at[stream, pl.ds(FROM_LINKS, OWN)],
            send_sem=near_send.at[panel],
            recv_sem=near_recv.at[panel],
            device_id=twin,
            device_id_type=MESH,
        )

    def sent(panel):
        for link in range(len(LINKS)):
            for to_core in range(2):
                to_link(link, to_core, panel, core).wait_send()
        to_twin(panel, core).wait_send()

    def send_panel(panel):
        if panel >= 2:
            sent(panel - 2)
        factor = 1.0 / SNPS if panel % 2 == 0 else 1.0

        def message(m, carry):
            to_core, link = m // len(LINKS), m % len(LINKS)
            step = step_of(link)
            block = wanted(device_at(step, to_core), panel)
            px, py, _ = place(step)
            kind = kind_of(block, px, py)
            for i in range(PER_LINK):
                slot = table_ref[kind, link * PER_LINK + i]
                away[link, to_core, panel % 2, i] = standard(slot, block & 1, factor)
            to_link(link, to_core, panel, core).start()
            return carry

        lax.fori_loop(0, 2 * len(LINKS), message, 0)
        for device in (twin, device_at(here, core)):
            block = wanted(device, panel)
            kind = kind_of(block, x, y)

            def one(i, carry):
                piece = standard(table_ref[kind, FROM_LINKS + i], block & 1, factor)
                if device is twin:
                    near[panel % 2, i] = piece
                else:
                    landed[panel][core, FROM_LINKS + i] = piece
                return carry

            lax.fori_loop(0, OWN, one, 0)
            if device is twin:
                to_twin(panel, core).start()

    for panel in range(PANELS):
        send_panel(panel)

    def in_order(panel, target):
        for link in range(len(LINKS)):
            for stream in range(STREAMS):
                to_link(link, 0, panel, stream).wait_recv()
        to_twin(panel, 1 - core).wait_recv()
        block = wanted(device_at(here, core), panel)
        live = pairs_ref[panel, device_at(here, core)[0] * COL_COUNT + device_at(here, core)[1]] >= 0
        keep = jnp.where(live, 1.0, 0.0).astype(jnp.bfloat16)
        dx = (x - lax.shift_right_logical(block, 1)) & (RING - 1)

        def one(col, carry):
            dy = (y - (2 * lax.shift_right_logical(block, 3) + col // RING)) & (RING - 1)
            dz = (z - col % RING) & (RING - 1)
            for p in range(PARTS):
                place = table_ref[16 + y % 2, p * RING**3 + (dx * RING + dy) * RING + dz]
                for stream in range(STREAMS):
                    first = col * SHARD + stream * (SHARD // 2) + p * PIECE
                    rows = pl.ds(pl.multiple_of(first, PIECE), PIECE)
                    piece = landed[panel][stream, place]
                    target[rows] = piece * keep if panel % 2 == 0 else piece
            return carry

        lax.fori_loop(0, COL_COUNT, one, 0)

    for p in range(PARTS):
        swap(p, core).wait_send()
    for step in RELAYS:
        for half in range(2):
            for item in step:
                relay(item, half).wait_send()
    in_order(0, left)
    in_order(1, right)

    def multiply(i, carry):
        rows = pl.ds(pl.multiple_of(i * CHUNK, CHUNK), CHUNK)
        product = lax.dot_general(
            left[rows], right[...], (((1,), (1,)), ((), ())), preferred_element_type=jnp.float32
        )
        tile_ref[rows] = product.astype(jnp.bfloat16)
        return carry

    lax.fori_loop(0, BLOCK // CHUNK, multiply, 0)
    in_order(2, panels_ref.at[0])
    in_order(3, panels_ref.at[1])
    for panel in (2, 3):
        sent(panel)


def gather(counts, pairs):
    dma = pltpu.SemaphoreType.DMA
    bf16 = jnp.bfloat16
    return pl.pallas_call(
        gather_kernel,
        out_shape=(
            jax.ShapeDtypeStruct((BLOCK, BLOCK), bf16),
            jax.ShapeDtypeStruct((2, BLOCK, SNPS), bf16),
        ),
        in_specs=[pl.BlockSpec(memory_space=pltpu.HBM)] * 3,
        out_specs=(pl.BlockSpec(memory_space=pltpu.VMEM),) * 2,
        scratch_shapes=[
            pltpu.VMEM((SHARD, SNPS), jnp.int32),
            pltpu.SMEM((PANELS, LANES), jnp.int32),
            pltpu.SMEM(TABLE.shape, jnp.int32),
            pltpu.VMEM((len(HELD), 2, PIECE, SNPS), bf16),
            pltpu.VMEM((15, 8, SNPS), jnp.int32),
            pltpu.VMEM((len(LINKS), 2, 2, PER_LINK, PIECE, SNPS), bf16),
            pltpu.VMEM((3, OWN, PIECE, SNPS), bf16),
            *[pltpu.VMEM((STREAMS, PIECES, PIECE, SNPS), bf16) for _ in range(PANELS)],
            pltpu.VMEM((BLOCK, SNPS), bf16),
            pltpu.VMEM((BLOCK, SNPS), bf16),
            dma((6,)),
            dma((PARTS,)),
            dma((PARTS,)),
            dma((len(HELD), 2)),
            dma((len(HELD), 2)),
            dma((15,)),
            dma((15,)),
            dma((len(LINKS), 2, PANELS)),
            dma((len(LINKS), 2, PANELS)),
            dma((PANELS,)),
            dma((PANELS,)),
        ],
        name="gather_panels",
        compiler_params=pltpu.CompilerParams(
            collective_id=0, has_side_effects=True, vmem_limit_bytes=36 * 2**20
        ),
    )(*(pltpu.with_memory_space_constraint(a, pltpu.HBM) for a in (counts, pairs, jnp.asarray(TABLE))))


def tile_kernel(tile_ref, panels_ref, out_ref, buffer, sem):
    first = pltpu.make_async_copy(tile_ref, out_ref.at[0, 0], sem.at[0])
    first.start()
    count = BLOCK // CHUNK

    def write(i):
        rows = pl.ds(i * CHUNK, CHUNK)
        return pltpu.make_async_copy(buffer.at[rows], out_ref.at[0, 1, rows], sem.at[1 + i])

    for i in range(count):
        rows = pl.ds(i * CHUNK, CHUNK)
        product = lax.dot_general(
            panels_ref[0, rows], panels_ref[1], (((1,), (1,)), ((), ())), preferred_element_type=jnp.float32
        )
        buffer[rows] = product.astype(jnp.bfloat16)
        write(i).start()
    first.wait()
    for i in range(count):
        write(i).wait()


def tiles(tile, panels):
    return pl.pallas_call(
        tile_kernel,
        out_shape=jax.ShapeDtypeStruct((1, 2, BLOCK, BLOCK), jnp.bfloat16),
        in_specs=[pl.BlockSpec(memory_space=pl.ANY), pl.BlockSpec(memory_space=pltpu.VMEM)],
        out_specs=pl.BlockSpec(memory_space=pl.ANY),
        scratch_shapes=[
            pltpu.VMEM((BLOCK, BLOCK), jnp.bfloat16),
            pltpu.SemaphoreType.DMA((1 + BLOCK // CHUNK,)),
        ],
        name="tile_products",
        compiler_params=pltpu.CompilerParams(vmem_limit_bytes=24 * 2**20),
    )(tile, panels)


def on_device(genotypes, pairs):
    by_panel = pairs.transpose(1, 2, 0).reshape(PANELS, -1)
    return tiles(*gather(genotypes, by_panel))


def solution(mesh):
    return jax.shard_map(
        on_device,
        mesh=mesh,
        in_specs=(P(("row", "col"), None), P()),
        out_specs=P(("row", "col"), None, None, None),
        check_vma=False,
    )
```

```python
import jax
import jax.numpy as jnp
import numpy as np
from jax import lax
from jax.experimental import pallas as pl
from jax.experimental.pallas import tpu as pltpu
from jax.sharding import PartitionSpec as P

MESH = pl.DeviceIdType.MESH
SNPS = 512
RING = 4
ROW_COUNT = 16
COL_COUNT = 8
SHARD = 256
SAMPLES = SHARD * ROW_COUNT * COL_COUNT
BLOCK = SHARD * COL_COUNT
STREAMS = 2
PARTS = 2
PIECE = SHARD // (STREAMS * PARTS)
PANELS = 4
LINKS = ((1, 0, 0), (3, 0, 0), (0, 1, 0), (0, 3, 0), (0, 0, 1), (0, 0, 3))
PER_LINK = 2
CHUNK = 512

RELAYS = (
    ((1, 16), (0, 48), (0, 4), (1, 12), (1, 1), (0, 3)),
    ((0, 20), (1, 60), (0, 52), (1, 28), (0, 49), (1, 19)),
    ((0, 36), (1, 44), (1, 5), (0, 15), (0, 21), (1, 63)),
    ((1, 35), (0, 33), (0, 24), (1, 56), (1, 29), (0, 55)),
    ((0, 40), (1, 40), (0, 25), (1, 59), (0, 34), (1, 34)),
    ((1, 11), (0, 9), (1, 38), (0, 46), (1, 30), (0, 54)),
)
DIRECT = (
    ((0, 1), (0, 6), (0, 19), (0, 31), (0, 37), (0, 41), (0, 56), (0, 62), (1, 8), (1, 15), (1, 21), (1, 27), (1, 32), (1, 45), (1, 50), (1, 54)),
    ((0, 5), (0, 8), (0, 18), (0, 30), (0, 32), (0, 39), (0, 57), (0, 63), (1, 3), (1, 14), (1, 22), (1, 24), (1, 43), (1, 47), (1, 49), (1, 53)),
    ((0, 13), (0, 28), (0, 29), (0, 38), (0, 44), (0, 58), (0, 59), (1, 4), (1, 9), (1, 20), (1, 23), (1, 42), (1, 48), (1, 51)),
    ((0, 11), (0, 12), (0, 16), (0, 17), (0, 42), (0, 60), (0, 61), (1, 7), (1, 25), (1, 26), (1, 36), (1, 46), (1, 52), (1, 55)),
    ((0, 10), (0, 22), (0, 26), (0, 35), (0, 47), (0, 50), (0, 53), (1, 2), (1, 6), (1, 13), (1, 17), (1, 39), (1, 41), (1, 57), (1, 61)),
    ((0, 2), (0, 7), (0, 14), (0, 23), (0, 27), (0, 43), (0, 45), (0, 51), (1, 10), (1, 18), (1, 31), (1, 33), (1, 37), (1, 58), (1, 62)),
)

ORDER = (
    0, 2, 4, 6, 8, 10, 1, 3, 5, 7, 9, 11, 18, 22, 16, 20, 12, 14,
    19, 23, 17, 21, 13, 15, 30, 29, 44, 36, 46, 38, 42, 40, 32, 37, 34, 39,
    43, 41, 33, 25, 35, 27, 31, 28, 45, 24, 58, 50, 52, 54, 57, 48, 59, 51,
    53, 55, 56, 49, 47, 26, 64, 69, 70, 62, 60, 67, 65, 68, 63, 61, 66, 71,
)


def offset_of(n):
    return n // (RING * RING), n // RING % RING, n % RING


def number(offset):
    return (offset[0] * RING + offset[1]) * RING + offset[2]


def before(n, link):
    return number(tuple((i - j) % RING for i, j in zip(offset_of(n), LINKS[link])))


HELD = tuple((p, 0) for p in range(PARTS)) + tuple(item for step in RELAYS for item in step)
LANES = 128
SLOT_OF = {item: i for i, item in enumerate(HELD)}
CAME_BY = {item: link for step in RELAYS for link, item in enumerate(step)}


def class_of(n, y_lo):
    dx, dy, _ = offset_of(n)
    return (dx * 2 + y_lo) * 2 + ((dy + 1 - y_lo) // 2) % 2


def tables():
    table = np.zeros((18, LANES), np.int32)
    own_most = 0
    for y_lo in range(2):
        for kind in sorted({class_of(n, y_lo) for n in range(RING**3)}):
            places = []
            for e, items in enumerate(DIRECT):
                mine = [(p, n) for p, n in items if class_of(n, y_lo) == kind]
                assert len(mine) <= PER_LINK
                places += [(e * PER_LINK + i, SLOT_OF[p, before(n, e)], p, n) for i, (p, n) in enumerate(mine)]
            own = [(slot, p, n) for slot, (p, n) in enumerate(HELD) if class_of(n, y_lo) == kind]
            own_most = max(own_most, len(own))
            places += [(FROM_LINKS + i, *one) for i, one in enumerate(own)]
            assert len(places) == PARTS * COL_COUNT
            for place, slot, p, n in places:
                table[kind, place] = slot
                table[16 + y_lo, p * RING**3 + n] = place
    return table, own_most


FROM_LINKS = len(LINKS) * PER_LINK
TABLE, OWN = tables()
PIECES = FROM_LINKS + OWN


def place_of_self():
    row, col = lax.axis_index("row"), lax.axis_index("col")
    return (row // 2) % RING, (row // 8) * 2 + col // RING, col % RING, row % 2


def kind_of(block, x, y):
    behind = (x - lax.shift_right_logical(block, 1)) & (RING - 1)
    half = ((y // 2) - lax.shift_right_logical(block, 3)) & 1
    return (behind * 2 + y % 2) * 2 + half


def gather_kernel(
    counts_hbm, pairs_hbm, table_hbm, tile_ref, panels_ref,
    counts_ref, pairs_ref, table_ref, held, sums, away, near, landed0, landed1, landed2, landed3, left, right,
    load_sem, twin_send, twin_recv, relay_send, relay_recv, stat_send, stat_recv,
    link_send, link_recv, near_send, near_recv,
):
    x, y, z, core = place_of_self()
    landed = (landed0, landed1, landed2, landed3)

    def place(offset):
        return tuple((me + step) % RING for me, step in zip((x, y, z), offset))

    def device_at(offset, on_core):
        px, py, pz = place(offset)
        return ((py // 2) * RING + px) * 2 + on_core, (py % 2) * RING + pz

    here = (0, 0, 0)
    twin = device_at(here, 1 - core)
    neighbours = [device_at(link, core) for link in LINKS]
    across = [device_at(tuple(2 * (a == axis) for a in range(3)), core) for axis in range(3)]
    others = [device_at(link, 1 - core) for link in LINKS]

    barrier = pltpu.get_barrier_semaphore()
    peers = [twin, *neighbours, *others, *across]
    for peer in peers:
        pl.semaphore_signal(barrier, inc=1, device_id=peer, device_id_type=MESH)

    mine, theirs = core * (SHARD // 2), (1 - core) * (SHARD // 2)
    quarters = [pl.ds(pl.multiple_of(half + p * PIECE, PIECE), PIECE) for half in (theirs, mine) for p in range(PARTS)]
    loads = [
        pltpu.make_async_copy(source, target, load_sem.at[i])
        for i, (source, target) in enumerate(
            [(counts_hbm.at[rows], counts_ref.at[rows]) for rows in quarters]
            + [(pairs_hbm, pairs_ref), (table_hbm, table_ref)]
        )
    ]
    for load in loads:
        load.start()
    for i, rows in enumerate(quarters):
        loads[i].wait()
        quarter = counts_ref[rows].astype(jnp.float32).astype(jnp.bfloat16)
        if i < PARTS:
            near[2, i] = quarter
        else:
            held[i - PARTS, core] = quarter
    halves = (core, 1 - core)

    def swap(p, half):
        return pltpu.make_async_remote_copy(
            src_ref=near.at[2, p],
            dst_ref=held.at[p, half],
            send_sem=twin_send.at[p],
            recv_sem=twin_recv.at[p],
            device_id=twin,
            device_id_type=MESH,
        )

    pl.semaphore_wait(barrier, len(peers))
    for p in range(PARTS):
        swap(p, core).start()

    def sum_to(slot, source, target):
        return pltpu.make_async_remote_copy(
            src_ref=sums.at[source],
            dst_ref=sums.at[slot],
            send_sem=stat_send.at[slot],
            recv_sem=stat_recv.at[slot],
            device_id=target,
            device_id_type=MESH,
        )

    def stat_copies(phase):
        if phase == 0:
            return [sum_to(1, 0, twin)]
        axis, base = phase - 1, 4 * phase - 2
        targets = [neighbours[2 * axis], neighbours[2 * axis + 1], across[axis]]
        return [sum_to(base + 1 + i, base, target) for i, target in enumerate(targets)]

    def stat_finish(phase):
        for copy in stat_copies(phase):
            copy.wait()
        if phase == 0:
            sums[2] = sums[0] + sums[1]
        else:
            base = 4 * phase - 2
            sums[base + 4] = (sums[base] + sums[base + 1]) + (sums[base + 2] + sums[base + 3])

    def stat_start():
        counts = counts_ref[...]
        total = jnp.sum(counts, axis=0, keepdims=True)
        square = jnp.sum(counts * counts, axis=0, keepdims=True)
        which = lax.broadcasted_iota(jnp.int32, (8, SNPS), 0)
        sums[0] = jnp.where(which == 0, total, jnp.where(which == 1, square, 0))
        for copy in stat_copies(0):
            copy.start()

    def relay(item, half):
        slot, link = SLOT_OF[item], CAME_BY[item]
        source = SLOT_OF[item[0], before(item[1], link)]
        return pltpu.make_async_remote_copy(
            src_ref=held.at[source, halves[half]],
            dst_ref=held.at[slot, halves[half]],
            send_sem=relay_send.at[slot, half],
            recv_sem=relay_recv.at[slot, half],
            device_id=neighbours[link],
            device_id_type=MESH,
        )

    arrived = {((p, 0), 0) for p in range(PARTS)}

    def arrive(item, half):
        if (item, half) not in arrived:
            arrived.add((item, half))
            if item[1] == 0:
                swap(item[0], halves[1]).wait_recv()
            else:
                relay(item, half).wait_recv()

    for i, code in enumerate(ORDER):
        item, half = HELD[PARTS + code // 2], code % 2
        arrive((item[0], before(item[1], CAME_BY[item])), half)
        relay(item, half).start()
        if i == len(LINKS) - 1:
            stat_start()
        t, last = divmod(i, 2 * len(LINKS))
        if last == 2 * len(LINKS) - 1 and 0 < t < 5:
            stat_finish(t - 1)
            if t < 4:
                for copy in stat_copies(t):
                    copy.start()
    for step in RELAYS:
        for half in range(2):
            for item in step:
                arrive(item, half)
    loads[4].wait()
    loads[5].wait()

    total, square = sums[14, 0:1], sums[14, 1:2]
    shifted = total - SAMPLES
    spread = SAMPLES * (square - 2 * total + SAMPLES) - shifted * shifted
    variance = spread.astype(jnp.float32) * (1.0 / (float(SAMPLES) * SAMPLES)) + 1e-05
    mean = total.astype(jnp.float32) * (1.0 / SAMPLES)
    scale = lax.rsqrt(variance)

    def standard(slot, half, factor):
        return ((held[slot, half].astype(jnp.float32) - mean) * (scale * factor)).astype(jnp.bfloat16)

    def wanted(device, panel):
        return jnp.maximum(pairs_ref[panel, device[0] * COL_COUNT + device[1]], 0)

    def step_of(link):
        step = 1 + 2 * (link % 2)
        return tuple(jnp.where(link // 2 == axis, step, 0) for axis in range(3))

    def to_link(link, to_core, panel, stream):
        return pltpu.make_async_remote_copy(
            src_ref=away.at[link, to_core, panel % 2],
            dst_ref=landed[panel].at[stream, pl.ds(link * PER_LINK, PER_LINK)],
            send_sem=link_send.at[link, to_core, panel],
            recv_sem=link_recv.at[link, stream, panel],
            device_id=device_at(step_of(link), to_core),
            device_id_type=MESH,
        )

    def to_twin(panel, stream):
        return pltpu.make_async_remote_copy(
            src_ref=near.at[panel % 2],
            dst_ref=landed[panel].at[stream, pl.ds(FROM_LINKS, OWN)],
            send_sem=near_send.at[panel],
            recv_sem=near_recv.at[panel],
            device_id=twin,
            device_id_type=MESH,
        )

    def sent(panel):
        for link in range(len(LINKS)):
            for to_core in range(2):
                to_link(link, to_core, panel, core).wait_send()
        to_twin(panel, core).wait_send()

    def send_panel(panel):
        if panel >= 2:
            sent(panel - 2)
        factor = 1.0 / SNPS if panel % 2 == 0 else 1.0

        def message(m, carry):
            to_core, link = (core + m // len(LINKS)) % 2, m % len(LINKS)
            step = step_of(link)
            block = wanted(device_at(step, to_core), panel)
            px, py, _ = place(step)
            kind = kind_of(block, px, py)
            for i in range(PER_LINK):
                slot = table_ref[kind, link * PER_LINK + i]
                away[link, to_core, panel % 2, i] = standard(slot, block & 1, factor)
            to_link(link, to_core, panel, core).start()
            return carry

        lax.fori_loop(0, 2 * len(LINKS), message, 0)
        for device in (twin, device_at(here, core)):
            block = wanted(device, panel)
            kind = kind_of(block, x, y)

            def one(i, carry):
                piece = standard(table_ref[kind, FROM_LINKS + i], block & 1, factor)
                if device is twin:
                    near[panel % 2, i] = piece
                else:
                    landed[panel][core, FROM_LINKS + i] = piece
                return carry

            lax.fori_loop(0, OWN, one, 0)
            if device is twin:
                to_twin(panel, core).start()

    for panel in range(PANELS):
        send_panel(panel)

    def in_order(panel, target):
        for link in range(len(LINKS)):
            for stream in range(STREAMS):
                to_link(link, 0, panel, stream).wait_recv()
        to_twin(panel, 1 - core).wait_recv()
        block = wanted(device_at(here, core), panel)
        live = pairs_ref[panel, device_at(here, core)[0] * COL_COUNT + device_at(here, core)[1]] >= 0
        keep = jnp.where(live, 1.0, 0.0).astype(jnp.bfloat16)
        dx = (x - lax.shift_right_logical(block, 1)) & (RING - 1)

        def one(col, carry):
            dy = (y - (2 * lax.shift_right_logical(block, 3) + col // RING)) & (RING - 1)
            dz = (z - col % RING) & (RING - 1)
            for p in range(PARTS):
                place = table_ref[16 + y % 2, p * RING**3 + (dx * RING + dy) * RING + dz]
                for stream in range(STREAMS):
                    first = col * SHARD + stream * (SHARD // 2) + p * PIECE
                    rows = pl.ds(pl.multiple_of(first, PIECE), PIECE)
                    piece = landed[panel][stream, place]
                    target[rows] = piece * keep if panel % 2 == 0 else piece
            return carry

        lax.fori_loop(0, COL_COUNT, one, 0)

    for p in range(PARTS):
        swap(p, core).wait_send()
    for step in RELAYS:
        for half in range(2):
            for item in step:
                relay(item, half).wait_send()
    in_order(0, left)
    in_order(1, right)

    def multiply(i, carry):
        rows = pl.ds(pl.multiple_of(i * CHUNK, CHUNK), CHUNK)
        product = lax.dot_general(
            left[rows], right[...], (((1,), (1,)), ((), ())), preferred_element_type=jnp.float32
        )
        tile_ref[rows] = product.astype(jnp.bfloat16)
        return carry

    lax.fori_loop(0, BLOCK // CHUNK, multiply, 0)
    in_order(2, panels_ref.at[0])
    in_order(3, panels_ref.at[1])
    for panel in (2, 3):
        sent(panel)


def gather(counts, pairs):
    dma = pltpu.SemaphoreType.DMA
    bf16 = jnp.bfloat16
    return pl.pallas_call(
        gather_kernel,
        out_shape=(
            jax.ShapeDtypeStruct((BLOCK, BLOCK), bf16),
            jax.ShapeDtypeStruct((2, BLOCK, SNPS), bf16),
        ),
        in_specs=[pl.BlockSpec(memory_space=pltpu.HBM)] * 3,
        out_specs=(pl.BlockSpec(memory_space=pltpu.VMEM),) * 2,
        scratch_shapes=[
            pltpu.VMEM((SHARD, SNPS), jnp.int32),
            pltpu.SMEM((PANELS, LANES), jnp.int32),
            pltpu.SMEM(TABLE.shape, jnp.int32),
            pltpu.VMEM((len(HELD), 2, PIECE, SNPS), bf16),
            pltpu.VMEM((15, 8, SNPS), jnp.int32),
            pltpu.VMEM((len(LINKS), 2, 2, PER_LINK, PIECE, SNPS), bf16),
            pltpu.VMEM((3, OWN, PIECE, SNPS), bf16),
            *[pltpu.VMEM((STREAMS, PIECES, PIECE, SNPS), bf16) for _ in range(PANELS)],
            pltpu.VMEM((BLOCK, SNPS), bf16),
            pltpu.VMEM((BLOCK, SNPS), bf16),
            dma((6,)),
            dma((PARTS,)),
            dma((PARTS,)),
            dma((len(HELD), 2)),
            dma((len(HELD), 2)),
            dma((15,)),
            dma((15,)),
            dma((len(LINKS), 2, PANELS)),
            dma((len(LINKS), 2, PANELS)),
            dma((PANELS,)),
            dma((PANELS,)),
        ],
        name="gather_panels",
        compiler_params=pltpu.CompilerParams(
            collective_id=0, has_side_effects=True, vmem_limit_bytes=36 * 2**20
        ),
    )(*(pltpu.with_memory_space_constraint(a, pltpu.HBM) for a in (counts, pairs, jnp.asarray(TABLE))))


def tile_kernel(tile_ref, panels_ref, out_ref, buffer, sem):
    first = pltpu.make_async_copy(tile_ref, out_ref.at[0, 0], sem.at[0])
    first.start()
    count = BLOCK // CHUNK

    def write(i):
        rows = pl.ds(i * CHUNK, CHUNK)
        return pltpu.make_async_copy(buffer.at[rows], out_ref.at[0, 1, rows], sem.at[1 + i])

    for i in range(count):
        rows = pl.ds(i * CHUNK, CHUNK)
        product = lax.dot_general(
            panels_ref[0, rows], panels_ref[1], (((1,), (1,)), ((), ())), preferred_element_type=jnp.float32
        )
        buffer[rows] = product.astype(jnp.bfloat16)
        write(i).start()
    first.wait()
    for i in range(count):
        write(i).wait()


def tiles(tile, panels):
    return pl.pallas_call(
        tile_kernel,
        out_shape=jax.ShapeDtypeStruct((1, 2, BLOCK, BLOCK), jnp.bfloat16),
        in_specs=[pl.BlockSpec(memory_space=pl.ANY), pl.BlockSpec(memory_space=pltpu.VMEM)],
        out_specs=pl.BlockSpec(memory_space=pl.ANY),
        scratch_shapes=[
            pltpu.VMEM((BLOCK, BLOCK), jnp.bfloat16),
            pltpu.SemaphoreType.DMA((1 + BLOCK // CHUNK,)),
        ],
        name="tile_products",
        compiler_params=pltpu.CompilerParams(vmem_limit_bytes=24 * 2**20),
    )(tile, panels)


def on_device(genotypes, pairs):
    by_panel = pairs.transpose(1, 2, 0).reshape(PANELS, -1)
    return tiles(*gather(genotypes, by_panel))


def solution(mesh):
    return jax.shard_map(
        on_device,
        mesh=mesh,
        in_specs=(P(("row", "col"), None), P()),
        out_specs=P(("row", "col"), None, None, None),
        check_vma=False,
    )
```

```python
import jax
import jax.numpy as jnp
import numpy as np
from jax import lax
from jax.experimental import pallas as pl
from jax.experimental.pallas import tpu as pltpu
from jax.sharding import PartitionSpec as P

MESH = pl.DeviceIdType.MESH
SNPS = 512
RING = 4
ROW_COUNT = 16
COL_COUNT = 8
SHARD = 256
SAMPLES = SHARD * ROW_COUNT * COL_COUNT
BLOCK = SHARD * COL_COUNT
STREAMS = 2
PARTS = 2
PIECE = SHARD // (STREAMS * PARTS)
PANELS = 4
LINKS = ((1, 0, 0), (3, 0, 0), (0, 1, 0), (0, 3, 0), (0, 0, 1), (0, 0, 3))
PER_LINK = 2
CHUNK = 512

RELAYS = (
    ((1, 16), (0, 48), (0, 4), (1, 12), (1, 1), (0, 3)),
    ((0, 20), (1, 60), (0, 52), (1, 28), (0, 49), (1, 19)),
    ((0, 36), (1, 44), (1, 5), (0, 15), (0, 21), (1, 63)),
    ((1, 35), (0, 33), (0, 24), (1, 56), (1, 29), (0, 55)),
    ((0, 40), (1, 40), (0, 25), (1, 59), (0, 34), (1, 34)),
    ((1, 11), (0, 9), (1, 38), (0, 46), (1, 30), (0, 54)),
)
DIRECT = (
    ((0, 1), (0, 6), (0, 19), (0, 31), (0, 37), (0, 41), (0, 56), (0, 62), (1, 8), (1, 15), (1, 21), (1, 27), (1, 32), (1, 45), (1, 50), (1, 54)),
    ((0, 5), (0, 8), (0, 18), (0, 30), (0, 32), (0, 39), (0, 57), (0, 63), (1, 3), (1, 14), (1, 22), (1, 24), (1, 43), (1, 47), (1, 49), (1, 53)),
    ((0, 13), (0, 28), (0, 29), (0, 38), (0, 44), (0, 58), (0, 59), (1, 4), (1, 9), (1, 20), (1, 23), (1, 42), (1, 48), (1, 51)),
    ((0, 11), (0, 12), (0, 16), (0, 17), (0, 42), (0, 60), (0, 61), (1, 7), (1, 25), (1, 26), (1, 36), (1, 46), (1, 52), (1, 55)),
    ((0, 10), (0, 22), (0, 26), (0, 35), (0, 47), (0, 50), (0, 53), (1, 2), (1, 6), (1, 13), (1, 17), (1, 39), (1, 41), (1, 57), (1, 61)),
    ((0, 2), (0, 7), (0, 14), (0, 23), (0, 27), (0, 43), (0, 45), (0, 51), (1, 10), (1, 18), (1, 31), (1, 33), (1, 37), (1, 58), (1, 62)),
)

ORDER = (
    0, 2, 4, 6, 8, 10, 1, 3, 5, 7, 9, 11, 18, 22, 16, 20, 12, 14,
    19, 23, 17, 21, 13, 15, 30, 29, 44, 36, 46, 38, 42, 40, 32, 37, 34, 39,
    43, 41, 33, 25, 35, 27, 31, 28, 45, 24, 58, 50, 52, 54, 57, 48, 59, 51,
    53, 55, 56, 49, 47, 26, 64, 69, 70, 62, 60, 67, 65, 68, 63, 61, 66, 71,
)


def offset_of(n):
    return n // (RING * RING), n // RING % RING, n % RING


def number(offset):
    return (offset[0] * RING + offset[1]) * RING + offset[2]


def before(n, link):
    return number(tuple((i - j) % RING for i, j in zip(offset_of(n), LINKS[link])))


HELD = tuple((p, 0) for p in range(PARTS)) + tuple(item for step in RELAYS for item in step)
LANES = 128
SLOT_OF = {item: i for i, item in enumerate(HELD)}
CAME_BY = {item: link for step in RELAYS for link, item in enumerate(step)}


def class_of(n, y_lo):
    dx, dy, _ = offset_of(n)
    return (dx * 2 + y_lo) * 2 + ((dy + 1 - y_lo) // 2) % 2


def tables():
    table = np.zeros((18, LANES), np.int32)
    own_most = 0
    for y_lo in range(2):
        for kind in sorted({class_of(n, y_lo) for n in range(RING**3)}):
            places = []
            for e, items in enumerate(DIRECT):
                mine = [(p, n) for p, n in items if class_of(n, y_lo) == kind]
                assert len(mine) <= PER_LINK
                places += [(e * PER_LINK + i, SLOT_OF[p, before(n, e)], p, n) for i, (p, n) in enumerate(mine)]
            own = [(slot, p, n) for slot, (p, n) in enumerate(HELD) if class_of(n, y_lo) == kind]
            own_most = max(own_most, len(own))
            places += [(FROM_LINKS + i, *one) for i, one in enumerate(own)]
            assert len(places) == PARTS * COL_COUNT
            for place, slot, p, n in places:
                table[kind, place] = slot
                table[16 + y_lo, p * RING**3 + n] = place
    return table, own_most


FROM_LINKS = len(LINKS) * PER_LINK
TABLE, OWN = tables()
PIECES = FROM_LINKS + OWN


def place_of_self():
    row, col = lax.axis_index("row"), lax.axis_index("col")
    return (row // 2) % RING, (row // 8) * 2 + col // RING, col % RING, row % 2


def kind_of(block, x, y):
    behind = (x - lax.shift_right_logical(block, 1)) & (RING - 1)
    half = ((y // 2) - lax.shift_right_logical(block, 3)) & 1
    return (behind * 2 + y % 2) * 2 + half


def gather_kernel(
    counts_hbm, pairs_hbm, table_hbm, tile_ref, panels_ref,
    counts_ref, pairs_ref, table_ref, held, sums, away, near, landed0, landed1, landed2, landed3, left, right,
    load_sem, twin_send, twin_recv, relay_send, relay_recv, stat_send, stat_recv,
    link_send, link_recv, near_send, near_recv,
):
    x, y, z, core = place_of_self()
    landed = (landed0, landed1, landed2, landed3)

    def place(offset):
        return tuple((me + step) % RING for me, step in zip((x, y, z), offset))

    def device_at(offset, on_core):
        px, py, pz = place(offset)
        return ((py // 2) * RING + px) * 2 + on_core, (py % 2) * RING + pz

    here = (0, 0, 0)
    twin = device_at(here, 1 - core)
    neighbours = [device_at(link, core) for link in LINKS]
    across = [device_at(tuple(2 * (a == axis) for a in range(3)), core) for axis in range(3)]
    others = [device_at(link, 1 - core) for link in LINKS]

    barrier = pltpu.get_barrier_semaphore()
    peers = [twin, *neighbours, *others, *across]
    for peer in peers:
        pl.semaphore_signal(barrier, inc=1, device_id=peer, device_id_type=MESH)

    mine, theirs = core * (SHARD // 2), (1 - core) * (SHARD // 2)
    quarters = [pl.ds(pl.multiple_of(half + p * PIECE, PIECE), PIECE) for half in (theirs, mine) for p in range(PARTS)]
    loads = [
        pltpu.make_async_copy(source, target, load_sem.at[i])
        for i, (source, target) in enumerate(
            [(counts_hbm.at[rows], counts_ref.at[rows]) for rows in quarters]
            + [(pairs_hbm, pairs_ref), (table_hbm, table_ref)]
        )
    ]
    for load in loads:
        load.start()
    for i, rows in enumerate(quarters):
        loads[i].wait()
        quarter = counts_ref[rows].astype(jnp.float32).astype(jnp.bfloat16)
        if i < PARTS:
            near[4, i] = quarter
        else:
            held[i - PARTS, core] = quarter
    halves = (core, 1 - core)

    def swap(p, half):
        return pltpu.make_async_remote_copy(
            src_ref=near.at[4, p],
            dst_ref=held.at[p, half],
            send_sem=twin_send.at[p],
            recv_sem=twin_recv.at[p],
            device_id=twin,
            device_id_type=MESH,
        )

    pl.semaphore_wait(barrier, len(peers))
    for p in range(PARTS):
        swap(p, core).start()

    def sum_to(slot, source, target):
        return pltpu.make_async_remote_copy(
            src_ref=sums.at[source],
            dst_ref=sums.at[slot],
            send_sem=stat_send.at[slot],
            recv_sem=stat_recv.at[slot],
            device_id=target,
            device_id_type=MESH,
        )

    def stat_copies(phase):
        if phase == 0:
            return [sum_to(1, 0, twin)]
        axis, base = phase - 1, 4 * phase - 2
        targets = [neighbours[2 * axis], neighbours[2 * axis + 1], across[axis]]
        return [sum_to(base + 1 + i, base, target) for i, target in enumerate(targets)]

    def stat_finish(phase):
        for copy in stat_copies(phase):
            copy.wait()
        if phase == 0:
            sums[2] = sums[0] + sums[1]
        else:
            base = 4 * phase - 2
            sums[base + 4] = (sums[base] + sums[base + 1]) + (sums[base + 2] + sums[base + 3])

    def stat_start():
        counts = counts_ref[...]
        total = jnp.sum(counts, axis=0, keepdims=True)
        square = jnp.sum(counts * counts, axis=0, keepdims=True)
        which = lax.broadcasted_iota(jnp.int32, (8, SNPS), 0)
        sums[0] = jnp.where(which == 0, total, jnp.where(which == 1, square, 0))
        for copy in stat_copies(0):
            copy.start()

    def relay(item, half):
        slot, link = SLOT_OF[item], CAME_BY[item]
        source = SLOT_OF[item[0], before(item[1], link)]
        return pltpu.make_async_remote_copy(
            src_ref=held.at[source, halves[half]],
            dst_ref=held.at[slot, halves[half]],
            send_sem=relay_send.at[slot, half],
            recv_sem=relay_recv.at[slot, half],
            device_id=neighbours[link],
            device_id_type=MESH,
        )

    arrived = {((p, 0), 0) for p in range(PARTS)}

    def arrive(item, half):
        if (item, half) not in arrived:
            arrived.add((item, half))
            if item[1] == 0:
                swap(item[0], halves[1]).wait_recv()
            else:
                relay(item, half).wait_recv()

    for i, code in enumerate(ORDER):
        item, half = HELD[PARTS + code // 2], code % 2
        arrive((item[0], before(item[1], CAME_BY[item])), half)
        relay(item, half).start()
        if i == len(LINKS) - 1:
            stat_start()
        t, last = divmod(i, 2 * len(LINKS))
        if last == 2 * len(LINKS) - 1 and 0 < t < 5:
            stat_finish(t - 1)
            if t < 4:
                for copy in stat_copies(t):
                    copy.start()
    for step in RELAYS:
        for half in range(2):
            for item in step:
                arrive(item, half)
    loads[4].wait()
    loads[5].wait()

    total, square = sums[14, 0:1], sums[14, 1:2]
    shifted = total - SAMPLES
    spread = SAMPLES * (square - 2 * total + SAMPLES) - shifted * shifted
    variance = spread.astype(jnp.float32) * (1.0 / (float(SAMPLES) * SAMPLES)) + 1e-05
    mean = total.astype(jnp.float32) * (1.0 / SAMPLES)
    scale = lax.rsqrt(variance)

    def standard(slot, half, factor):
        return ((held[slot, half].astype(jnp.float32) - mean) * (scale * factor)).astype(jnp.bfloat16)

    def wanted(device, panel):
        return jnp.maximum(pairs_ref[panel, device[0] * COL_COUNT + device[1]], 0)

    def step_of(link):
        step = 1 + 2 * (link % 2)
        return tuple(jnp.where(link // 2 == axis, step, 0) for axis in range(3))

    def to_link(link, to_core, panel, stream):
        return pltpu.make_async_remote_copy(
            src_ref=away.at[link, to_core, panel],
            dst_ref=landed[panel].at[stream, pl.ds(link * PER_LINK, PER_LINK)],
            send_sem=link_send.at[link, to_core, panel],
            recv_sem=link_recv.at[link, stream, panel],
            device_id=device_at(step_of(link), to_core),
            device_id_type=MESH,
        )

    def to_twin(panel, stream):
        return pltpu.make_async_remote_copy(
            src_ref=near.at[panel],
            dst_ref=landed[panel].at[stream, pl.ds(FROM_LINKS, OWN)],
            send_sem=near_send.at[panel],
            recv_sem=near_recv.at[panel],
            device_id=twin,
            device_id_type=MESH,
        )

    def sent(panel):
        for link in range(len(LINKS)):
            for to_core in range(2):
                to_link(link, to_core, panel, core).wait_send()
        to_twin(panel, core).wait_send()

    def send_panel(panel):
        factor = 1.0 / SNPS if panel % 2 == 0 else 1.0

        def message(m, carry):
            to_core, link = (core + m // len(LINKS)) % 2, m % len(LINKS)
            step = step_of(link)
            block = wanted(device_at(step, to_core), panel)
            px, py, _ = place(step)
            kind = kind_of(block, px, py)
            for i in range(PER_LINK):
                slot = table_ref[kind, link * PER_LINK + i]
                away[link, to_core, panel, i] = standard(slot, block & 1, factor)
            to_link(link, to_core, panel, core).start()
            return carry

        lax.fori_loop(0, 2 * len(LINKS), message, 0)
        for device in (twin, device_at(here, core)):
            block = wanted(device, panel)
            kind = kind_of(block, x, y)

            def one(i, carry):
                piece = standard(table_ref[kind, FROM_LINKS + i], block & 1, factor)
                if device is twin:
                    near[panel, i] = piece
                else:
                    landed[panel][core, FROM_LINKS + i] = piece
                return carry

            lax.fori_loop(0, OWN, one, 0)
            if device is twin:
                to_twin(panel, core).start()

    for panel in range(PANELS):
        send_panel(panel)

    def in_order(panel, target):
        for link in range(len(LINKS)):
            for stream in range(STREAMS):
                to_link(link, 0, panel, stream).wait_recv()
        to_twin(panel, 1 - core).wait_recv()
        block = wanted(device_at(here, core), panel)
        live = pairs_ref[panel, device_at(here, core)[0] * COL_COUNT + device_at(here, core)[1]] >= 0
        keep = jnp.where(live, 1.0, 0.0).astype(jnp.bfloat16)
        dx = (x - lax.shift_right_logical(block, 1)) & (RING - 1)

        def one(col, carry):
            dy = (y - (2 * lax.shift_right_logical(block, 3) + col // RING)) & (RING - 1)
            dz = (z - col % RING) & (RING - 1)
            for p in range(PARTS):
                place = table_ref[16 + y % 2, p * RING**3 + (dx * RING + dy) * RING + dz]
                for stream in range(STREAMS):
                    first = col * SHARD + stream * (SHARD // 2) + p * PIECE
                    rows = pl.ds(pl.multiple_of(first, PIECE), PIECE)
                    piece = landed[panel][stream, place]
                    target[rows] = piece * keep if panel % 2 == 0 else piece
            return carry

        lax.fori_loop(0, COL_COUNT, one, 0)

    for p in range(PARTS):
        swap(p, core).wait_send()
    for step in RELAYS:
        for half in range(2):
            for item in step:
                relay(item, half).wait_send()
    in_order(0, left)
    in_order(1, right)

    def multiply(i, carry):
        rows = pl.ds(pl.multiple_of(i * CHUNK, CHUNK), CHUNK)
        product = lax.dot_general(
            left[rows], right[...], (((1,), (1,)), ((), ())), preferred_element_type=jnp.float32
        )
        tile_ref[rows] = product.astype(jnp.bfloat16)
        return carry

    lax.fori_loop(0, BLOCK // CHUNK, multiply, 0)
    in_order(2, panels_ref.at[0])
    in_order(3, panels_ref.at[1])
    for panel in range(PANELS):
        sent(panel)


def gather(counts, pairs):
    dma = pltpu.SemaphoreType.DMA
    bf16 = jnp.bfloat16
    return pl.pallas_call(
        gather_kernel,
        out_shape=(
            jax.ShapeDtypeStruct((BLOCK, BLOCK), bf16),
            jax.ShapeDtypeStruct((2, BLOCK, SNPS), bf16),
        ),
        in_specs=[pl.BlockSpec(memory_space=pltpu.HBM)] * 3,
        out_specs=(pl.BlockSpec(memory_space=pltpu.VMEM),) * 2,
        scratch_shapes=[
            pltpu.VMEM((SHARD, SNPS), jnp.int32),
            pltpu.SMEM((PANELS, LANES), jnp.int32),
            pltpu.SMEM(TABLE.shape, jnp.int32),
            pltpu.VMEM((len(HELD), 2, PIECE, SNPS), bf16),
            pltpu.VMEM((15, 8, SNPS), jnp.int32),
            pltpu.VMEM((len(LINKS), 2, PANELS, PER_LINK, PIECE, SNPS), bf16),
            pltpu.VMEM((PANELS + 1, OWN, PIECE, SNPS), bf16),
            *[pltpu.VMEM((STREAMS, PIECES, PIECE, SNPS), bf16) for _ in range(PANELS)],
            pltpu.VMEM((BLOCK, SNPS), bf16),
            pltpu.VMEM((BLOCK, SNPS), bf16),
            dma((6,)),
            dma((PARTS,)),
            dma((PARTS,)),
            dma((len(HELD), 2)),
            dma((len(HELD), 2)),
            dma((15,)),
            dma((15,)),
            dma((len(LINKS), 2, PANELS)),
            dma((len(LINKS), 2, PANELS)),
            dma((PANELS,)),
            dma((PANELS,)),
        ],
        name="gather_panels",
        compiler_params=pltpu.CompilerParams(
            collective_id=0, has_side_effects=True, vmem_limit_bytes=40 * 2**20
        ),
    )(*(pltpu.with_memory_space_constraint(a, pltpu.HBM) for a in (counts, pairs, jnp.asarray(TABLE))))


def tile_kernel(tile_ref, panels_ref, out_ref, buffer, sem):
    first = pltpu.make_async_copy(tile_ref, out_ref.at[0, 0], sem.at[0])
    first.start()
    count = BLOCK // CHUNK

    def write(i):
        rows = pl.ds(i * CHUNK, CHUNK)
        return pltpu.make_async_copy(buffer.at[rows], out_ref.at[0, 1, rows], sem.at[1 + i])

    for i in range(count):
        rows = pl.ds(i * CHUNK, CHUNK)
        product = lax.dot_general(
            panels_ref[0, rows], panels_ref[1], (((1,), (1,)), ((), ())), preferred_element_type=jnp.float32
        )
        buffer[rows] = product.astype(jnp.bfloat16)
        write(i).start()
    first.wait()
    for i in range(count):
        write(i).wait()


def tiles(tile, panels):
    return pl.pallas_call(
        tile_kernel,
        out_shape=jax.ShapeDtypeStruct((1, 2, BLOCK, BLOCK), jnp.bfloat16),
        in_specs=[pl.BlockSpec(memory_space=pl.ANY), pl.BlockSpec(memory_space=pltpu.VMEM)],
        out_specs=pl.BlockSpec(memory_space=pl.ANY),
        scratch_shapes=[
            pltpu.VMEM((BLOCK, BLOCK), jnp.bfloat16),
            pltpu.SemaphoreType.DMA((1 + BLOCK // CHUNK,)),
        ],
        name="tile_products",
        compiler_params=pltpu.CompilerParams(vmem_limit_bytes=24 * 2**20),
    )(tile, panels)


def on_device(genotypes, pairs):
    by_panel = pairs.transpose(1, 2, 0).reshape(PANELS, -1)
    return tiles(*gather(genotypes, by_panel))


def solution(mesh):
    return jax.shard_map(
        on_device,
        mesh=mesh,
        in_specs=(P(("row", "col"), None), P()),
        out_specs=P(("row", "col"), None, None, None),
        check_vma=False,
    )
```
